32 devices in a mesh: fsdp: 4 (over y, x), ctx: 8 (over z, core).
Axes of the slice: x: 2, y: 2, z: 4, core: 2. Of those that a mesh axis runs over, the one named last changes fastest.
Arguments:
- tokens: bfloat16 [4, 1024, 1024], P('fsdp', 'ctx'), may hold values from -16 to 16
- cotangent: bfloat16 [4, 1024, 1024], P('fsdp', 'ctx'), may hold values from -6 to 6
- w_query: bfloat16 [1024, 512], P('fsdp')
- w_key: bfloat16 [1024, 512], P('fsdp')
- w_value: bfloat16 [1024, 512], P('fsdp'), may hold values from -0.1875 to 0.1875
- w_out: bfloat16 [512, 1024], P('fsdp'), may hold values from -0.25 to 0.25
- block_mask: int32 [8, 8], replicated, may hold values from 0 to 1, as said below
- span_order: int32 [16], replicated, may hold values from 0 to 15, each once
Outputs:
- mixed_out: bfloat16 [4, 1024, 1024], P('fsdp', 'ctx')
- token_grad: bfloat16 [4, 1024, 1024], P('fsdp', 'ctx')
- grad_query: float32 [1024, 512], P(('fsdp', 'ctx'))
- grad_key: float32 [1024, 512], P(('fsdp', 'ctx'))
- grad_value: float32 [1024, 512], P(('fsdp', 'ctx'))
- grad_out: float32 [512, 1024], P(('fsdp', 'ctx'))
The draws below stay inside these ranges and needn't reach their ends.
Inputs may be any that keep to these rules, and one draw needn't show every extreme that they name: `block_mask`: every diagonal entry is 1.
All inputs are finite; a program needn't handle non-finite values.
Results may differ from the reference program's by a relative error of at most 0.013.
The reference program's roundings to bfloat16 on the way (of `attention` and `d_attention`) count: a program that leaves them out, or rounds other values in their place, can miss the bound.
Values may be sent and summed in bfloat16 or wider, within the bound.
A program may use at most 128 MiB of HBM per device.

```python
from functools import partial
import jax
import jax.numpy as jnp
from jax import lax

D = 1024
HEADS = 4
HD = 128
BLK = 128
SPAN = 64
HQ = 512
SEQ = 1024
NB = 8
NCH = 16
CLIPS = 4


def projection_base(key):
    return jax.random.normal(jax.random.fold_in(key, 101), (D, HQ), jnp.float32) / D ** 0.5


def draw_w_query(key, part):
    return projection_base(key).astype(jnp.bfloat16)


def draw_w_key(key, part):
    others = jax.random.normal(jax.random.fold_in(key, 202), (D, HQ), jnp.float32) / D ** 0.5
    return others.astype(jnp.bfloat16)


def draw_tokens(key, part):
    base = jax.random.normal(jax.random.fold_in(key, 303), (CLIPS, SEQ, D), jnp.float32)
    return jnp.clip(base, -6.0, 6.0).astype(jnp.bfloat16)


def draw_block_mask(key, part):
    bits = jax.random.randint(jax.random.fold_in(key, 405), (NB, NB), 0, 2, dtype=jnp.int32)
    lanes = jnp.arange(NB, dtype=jnp.int32)
    diagonal = (lanes[:, None] == lanes[None, :]).astype(jnp.int32)
    return jnp.maximum(bits, diagonal)


def steps_of(stream_key, shape, shards, least, top_value):
    def one(dim, shards_of):
        heights = jax.random.uniform(jax.random.fold_in(jax.random.fold_in(stream_key, 6), dim), (shards_of,), jnp.float32, least / len(shards), top_value / len(shards))
        return jnp.repeat(jnp.exp(heights), shape[dim] // shards_of).reshape((-1,) + (1,) * (len(shape) - dim - 1))

    factor_of = one(*shards[0])
    for cut in shards[1:]:
        factor_of = factor_of * one(*cut)
    return factor_of


def normal_values(stream_key, extent, scale, limit, shards=(), kind=jnp.bfloat16):
    loudness = steps_of(stream_key, extent, shards, -0.22, 0.18) if shards else 1.0
    values = jax.random.normal(stream_key, extent, jnp.float32) * scale * loudness
    return jnp.minimum(jnp.maximum(values, -limit), limit).astype(kind)


def setup_inputs(seed: int = 0) -> dict:
    key_of = jax.random.split(jax.random.key(seed), 9)
    return {
        "tokens": draw_tokens(jax.random.fold_in(key_of[8], 71), 0),
        "cotangent": normal_values(key_of[1], (CLIPS, SEQ, D), 1.0, 6.0, ((0, 4), (1, 8))),
        "w_query": draw_w_query(jax.random.fold_in(key_of[8], 71), 0),
        "w_key": draw_w_key(jax.random.fold_in(key_of[8], 71), 0),
        "w_value": normal_values(key_of[4], (D, HQ), D ** -0.5, 0.1875, ((0, 4),)),
        "w_out": normal_values(key_of[5], (HQ, D), HQ ** -0.5, 0.25, ((0, 4),)),
        "block_mask": draw_block_mask(jax.random.fold_in(key_of[8], 71), 0),
        "span_order": jax.random.permutation(key_of[7], NCH).astype(jnp.int32),
    }


NEG = -1e+30

def stored_blocks(span_order):
    rows = jnp.arange(SEQ, dtype=jnp.int32)
    first = span_order[rows // SPAN].astype(jnp.int32)
    return (first * SPAN + rows % SPAN) // BLK

def attend(allowed, qf, kf, vf):
    scale = 1.0 / HD ** 0.5
    score = jnp.einsum('qhd,khd->hqk', qf, kf, precision=lax.Precision.HIGHEST) * scale
    score = jnp.where(allowed[None], score, NEG)
    top = lax.stop_gradient(lax.optimization_barrier(jnp.max(score, axis=-1, keepdims=True)))
    prob = jnp.where(allowed[None], jnp.exp(score - top), 0.0)
    prob = prob / lax.optimization_barrier(jnp.sum(prob, axis=-1, keepdims=True))
    return jnp.einsum('hqk,khd->qhd', prob, vf, precision=lax.Precision.HIGHEST)

def one_clip(x, dy, allowed, w_query, w_key, w_value, w_out):
    shape3 = (SEQ, HEADS, HD)
    query = jnp.dot(x, w_query, preferred_element_type=jnp.float32).astype(jnp.bfloat16)
    keys = jnp.dot(x, w_key, preferred_element_type=jnp.float32).astype(jnp.bfloat16)
    values = jnp.dot(x, w_value, preferred_element_type=jnp.float32).astype(jnp.bfloat16)
    qf = query.astype(jnp.float32).reshape(shape3)
    kf = keys.astype(jnp.float32).reshape(shape3)
    vf = values.astype(jnp.float32).reshape(shape3)
    combined, pull = jax.vjp(partial(attend, allowed), qf, kf, vf)
    attention = combined.reshape(SEQ, HQ).astype(jnp.bfloat16)
    mixed = (x.astype(jnp.float32) + jnp.dot(attention, w_out, preferred_element_type=jnp.float32)).astype(jnp.bfloat16)
    d_attention = jnp.dot(dy, w_out.T, preferred_element_type=jnp.float32).astype(jnp.bfloat16)
    d_query, d_key, d_value = pull(d_attention.astype(jnp.float32).reshape(shape3))
    d_query = d_query.reshape(SEQ, HQ).astype(jnp.bfloat16)
    d_key = d_key.reshape(SEQ, HQ).astype(jnp.bfloat16)
    d_value = d_value.reshape(SEQ, HQ).astype(jnp.bfloat16)
    token_grad = (dy.astype(jnp.float32) + jnp.dot(d_query, w_query.T, preferred_element_type=jnp.float32) + jnp.dot(d_key, w_key.T, preferred_element_type=jnp.float32) + jnp.dot(d_value, w_value.T, preferred_element_type=jnp.float32)).astype(jnp.bfloat16)
    grad_query = jnp.dot(x.T, d_query, preferred_element_type=jnp.float32)
    grad_key = jnp.dot(x.T, d_key, preferred_element_type=jnp.float32)
    grad_value = jnp.dot(x.T, d_value, preferred_element_type=jnp.float32)
    grad_out = jnp.dot(attention.T, dy, preferred_element_type=jnp.float32)
    return (mixed, token_grad, grad_query, grad_key, grad_value, grad_out)

def reference(tokens, cotangent, w_query, w_key, w_value, w_out, block_mask, span_order):
    block = stored_blocks(span_order)
    allowed = block_mask[block][:, block] == 1

    def per_clip(item):
        return one_clip(item[0], item[1], allowed, w_query, w_key, w_value, w_out)
    mixed, token_grad, grad_query, grad_key, grad_value, grad_out = lax.map(per_clip, (tokens, cotangent))
    return (mixed, token_grad, lax.optimization_barrier(jnp.sum(grad_query, axis=0)), lax.optimization_barrier(jnp.sum(grad_key, axis=0)), lax.optimization_barrier(jnp.sum(grad_value, axis=0)), lax.optimization_barrier(jnp.sum(grad_out, axis=0)))
```

```python
import functools
import math

import jax
import jax.numpy as jnp
from jax import lax
from jax.experimental import pallas as pl
from jax.experimental.pallas import tpu as pltpu
from jax.sharding import PartitionSpec as P

HEADS = 4
HD = 128
BLK = 128
SPAN = 64


NEG = -1e30
HIGH = lax.Precision.HIGHEST


def block_ids(span_order, start, count):
    rows = start + jnp.arange(count, dtype=jnp.int32)
    span = rows // SPAN
    lanes = jnp.arange(span_order.shape[0], dtype=jnp.int32)
    first = jnp.sum(jnp.where(span[:, None] == lanes[None, :], span_order[None, :], 0), axis=1)
    return (first * SPAN + rows % SPAN) // BLK


def allowed_between(mask_f, row_ids, col_ids):
    lanes = jnp.arange(mask_f.shape[0], dtype=jnp.int32)
    left = (row_ids[:, None] == lanes[None, :]).astype(jnp.float32)
    right = (col_ids[:, None] == lanes[None, :]).astype(jnp.float32)
    linked = jnp.dot(jnp.dot(left, mask_f), right.T)
    return linked > 0.5


def over_blocks(step, carry, pieces):
    count = pieces[0].shape[0]
    width = 512
    stacked = tuple((piece.reshape((count // width, width) + piece.shape[1:]) for piece in pieces))

    def scan_step(state, item):
        number, parts = item
        return (step(state, parts, number * width), None)

    numbers = jnp.arange(count // width, dtype=jnp.int32)
    carry, _ = lax.scan(scan_step, carry, (numbers, stacked))
    return carry


def contract_rows(left, right):
    return lax.dot_general(
        left, right, (((0,), (0,)), ((), ())), preferred_element_type=jnp.float32
    )


def contract_cols(left, right):
    return lax.dot_general(
        left, right, (((1,), (1,)), ((), ())), preferred_element_type=jnp.float32
    )


def body(tokens, cotangent, w_query, w_key, w_value, w_out, block_mask, span_order):
    x_rows = tokens[0]
    dy_rows = cotangent[0]
    rows = x_rows.shape[0]
    scale = 1.0 / math.sqrt(HD)
    full_q, full_k, full_v, full_o = (
        lax.all_gather(w_query, "fsdp", axis=0, tiled=True),
        lax.all_gather(w_key, "fsdp", axis=0, tiled=True),
        lax.all_gather(w_value, "fsdp", axis=0, tiled=True),
        lax.all_gather(w_out, "fsdp", axis=0, tiled=True),
    )
    query = jnp.dot(x_rows, full_q, preferred_element_type=jnp.float32).astype(jnp.bfloat16)
    keys = jnp.dot(x_rows, full_k, preferred_element_type=jnp.float32).astype(jnp.bfloat16)
    values = jnp.dot(x_rows, full_v, preferred_element_type=jnp.float32).astype(jnp.bfloat16)
    d_attn = contract_cols(dy_rows, full_o).astype(jnp.bfloat16)
    mask_f = block_mask.astype(jnp.float32)
    own_ids = block_ids(span_order, lax.axis_index("ctx") * rows, rows)
    q_own = query.reshape(rows, HEADS, HD)
    k_own = keys.reshape(rows, HEADS, HD)
    v_own = values.reshape(rows, HEADS, HD)
    g_own = d_attn.reshape(rows, HEADS, HD)

    def sweep_keys(carry, parts, start):
        top, total, out_acc, mix_acc, key_acc, dot_acc = carry
        count = parts[0].shape[0]
        k_part = parts[0].reshape(count, HEADS, HD)
        v_part = parts[1].reshape(count, HEADS, HD)
        keep = allowed_between(mask_f, own_ids, block_ids(span_order, start, count))[None]
        score = (
            jnp.einsum("qhd,khd->hqk", q_own, k_part, preferred_element_type=jnp.float32) * scale
        )
        score = jnp.where(keep, score, NEG)
        new_top = jnp.maximum(top, jnp.max(score, axis=-1))
        fade = jnp.exp(top - new_top)
        prob = jnp.where(keep, jnp.exp(score - new_top[:, :, None]), 0.0)
        k_wide = k_part.astype(jnp.float32)
        v_wide = v_part.astype(jnp.float32)
        total = fade * total + jnp.sum(prob, axis=-1)
        out_acc = fade[:, :, None] * out_acc + jnp.einsum(
            "hqk,khd->hqd", prob, v_wide, precision=HIGH
        )
        d_prob = jnp.einsum("qhd,khd->hqk", g_own, v_part, preferred_element_type=jnp.float32)
        weighted = prob * d_prob
        dot_acc = fade * dot_acc + jnp.sum(weighted, axis=-1)
        mix_acc = fade[:, :, None] * mix_acc + jnp.einsum(
            "hqk,khd->hqd", weighted, k_wide, precision=HIGH
        )
        key_acc = fade[:, :, None] * key_acc + jnp.einsum(
            "hqk,khd->hqd", prob, k_wide, precision=HIGH
        )
        return (new_top, total, out_acc, mix_acc, key_acc, dot_acc)

    flat = jnp.zeros((HEADS, rows), jnp.float32)
    cube = jnp.zeros((HEADS, rows, HD), jnp.float32)
    begin = (jnp.full((HEADS, rows), NEG, jnp.float32), flat, cube, cube, cube, flat)
    top, total, out_acc, mix_acc, key_acc, dot_acc = over_blocks(
        sweep_keys,
        begin,
        (
            lax.all_gather(keys, "ctx", axis=0, tiled=True),
            lax.all_gather(values, "ctx", axis=0, tiled=True),
        ),
    )
    share = 1.0 / total
    combined = out_acc * share[:, :, None]
    log_total = top + jnp.log(total)
    attention = jnp.transpose(combined, (1, 0, 2)).reshape(rows, HEADS * HD).astype(jnp.bfloat16)
    mixed = (
        x_rows.astype(jnp.float32) + jnp.dot(attention, full_o, preferred_element_type=jnp.float32)
    ).astype(jnp.bfloat16)
    delta = dot_acc * share
    log_rows = jnp.transpose(log_total)
    delta_rows = jnp.transpose(delta)

    def key_side(acc, parts, start):
        d_key, d_value = acc
        count = parts[0].shape[0]
        q_part = parts[0].reshape(count, HEADS, HD)
        g_part = parts[1].reshape(count, HEADS, HD)
        lse_part = jnp.transpose(parts[2])
        delta_part = jnp.transpose(parts[3])
        keep = allowed_between(mask_f, block_ids(span_order, start, count), own_ids)[None]
        score = (
            jnp.einsum("khd,qhd->hkq", q_part, k_own, preferred_element_type=jnp.float32) * scale
        )
        score = jnp.where(keep, score, NEG)
        prob = jnp.where(keep, jnp.exp(score - lse_part[:, :, None]), 0.0)
        d_prob = jnp.einsum("khd,qhd->hkq", g_part, v_own, preferred_element_type=jnp.float32)
        d_score = prob * (d_prob - delta_part[:, :, None])
        d_key = d_key + scale * jnp.einsum(
            "hkq,khd->hqd", d_score, q_part.astype(jnp.float32), precision=HIGH
        )
        d_value = d_value + jnp.einsum(
            "hkq,khd->hqd", prob, g_part.astype(jnp.float32), precision=HIGH
        )
        return (d_key, d_value)

    d_query = scale * (mix_acc - delta[:, :, None] * key_acc) * share[:, :, None]
    d_key, d_value = over_blocks(
        key_side,
        (cube, cube),
        (
            lax.all_gather(query.astype(jnp.float32), "ctx", axis=0, tiled=True).astype(
                jnp.bfloat16
            ),
            lax.all_gather(d_attn.astype(jnp.float32), "ctx", axis=0, tiled=True).astype(
                jnp.bfloat16
            ),
            lax.all_gather(log_rows, "ctx", axis=0, tiled=True),
            lax.all_gather(delta_rows, "ctx", axis=0, tiled=True),
        ),
    )

    def to_rows(grad_heads):
        return jnp.transpose(grad_heads, (1, 0, 2)).reshape(rows, HEADS * HD).astype(jnp.bfloat16)

    dq_rows = to_rows(d_query)
    dk_rows = to_rows(d_key)
    dv_rows = to_rows(d_value)
    token_grad = (
        dy_rows.astype(jnp.float32)
        + contract_cols(dq_rows, full_q)
        + contract_cols(dk_rows, full_k)
        + contract_cols(dv_rows, full_v)
    ).astype(jnp.bfloat16)
    grad_q = contract_rows(x_rows, dq_rows)
    grad_k = contract_rows(x_rows, dk_rows)
    grad_v = contract_rows(x_rows, dv_rows)
    grad_o = contract_rows(attention, dy_rows)
    grad_q, grad_k, grad_v, grad_o = (
        lax.psum_scatter(grad_q, ("fsdp", "ctx"), scatter_dimension=0, tiled=True),
        lax.psum_scatter(grad_k, ("fsdp", "ctx"), scatter_dimension=0, tiled=True),
        lax.psum_scatter(grad_v, ("fsdp", "ctx"), scatter_dimension=0, tiled=True),
        lax.psum_scatter(grad_o, ("fsdp", "ctx"), scatter_dimension=0, tiled=True),
    )
    return (mixed[None], token_grad[None], grad_q, grad_k, grad_v, grad_o)


def dot_rows(left, right):
    return lax.dot_general(
        left, right, (((0,), (0,)), ((), ())), preferred_element_type=jnp.float32
    )


def dot_plain(left, right):
    return jnp.dot(left, right, preferred_element_type=jnp.float32)


def fused_kernel(
    F,
    x_ref, dy_ref, wq_ref, wk_ref, wv_ref, wo_ref, bias_ref,
    mixed_ref, token_ref, gq_ref, gk_ref, gv_ref, go_ref,
    xg, wq_all, wk_all, wv_all, wo_all, wh, g_send, g_got, kv_buf, q_buf,
    att_send, att_own, dq_send, dq_own, dkv_acc, dkv_pair, dkv_send, dkv_own, d_head,
    go0, go0_got, go1, go1_got, go2, go2_got,
    gw0, gw0_got, gw1, gw1_got, gw2, gw2_got,
    x_s, x_r, xf_s, xf_r, w_s, w_r, wf_s, wf_r, g_s, g_r, at_s, at_r, dq_s, dq_r,
    dk_s, dk_r, pair_s, pair_r, go1_s, go1_r, go2_s, go2_r, gw1_s, gw1_r, gw2_s, gw2_r,
):
    H = HEADS
    f = lax.axis_index("fsdp")
    ctx = lax.axis_index("ctx")
    z = ctx // 2
    c = ctx % 2
    other = 1 - c
    rows = x_ref.shape[0]
    bf = jnp.bfloat16
    f32 = jnp.float32
    scale = 1.0 / math.sqrt(HD)

    pair_dev = (f, z * 2 + other)

    def head_dev(k):
        return (f, lax.rem(z + k, H) * 2 + c)

    def clip_dev(k):
        return (lax.rem(f + k, F), ctx)

    started = []

    def send(src, dst, s, r, dev):
        copy = pltpu.make_async_remote_copy(
            src_ref=src, dst_ref=dst, send_sem=s, recv_sem=r,
            device_id=dev, device_id_type=pl.DeviceIdType.MESH,
        )
        copy.start()
        started.append(copy)
        return copy

    barrier = pltpu.get_barrier_semaphore()
    peers = [pair_dev] + [head_dev(k) for k in range(1, H)] + [clip_dev(k) for k in range(1, F)]
    for dev in peers:
        pl.semaphore_signal(barrier, inc=1, device_id=dev, device_id_type=pl.DeviceIdType.MESH)
    pl.semaphore_wait(barrier, len(peers))

    weights = ((wo_ref, wo_all), (wk_ref, wk_all), (wv_ref, wv_all), (wq_ref, wq_all))

    def half_of(i, owner, part):
        n = weights[i][0].shape[0]
        start = pl.multiple_of(owner * n + part * (n // 2), n // 2)
        return weights[i][1].at[pl.ds(start, n // 2)]

    def w_send(i):
        ref = weights[i][0]
        n = ref.shape[0] // 2
        src = ref.at[pl.ds(pl.multiple_of(c * n, n), n)]
        return [
            send(src, half_of(i, f, c), w_s.at[i, k - 1], w_r.at[i, k - 1], clip_dev(k))
            for k in range(1, F)
        ]

    w_copies = [w_send(0)]
    x_copies = [
        send(x_ref, xg.at[c, z], x_s.at[k - 1], x_r.at[k - 1], head_dev(k)) for k in range(1, H)
    ]
    x_pair = [send(x_ref, xg.at[c, z], xf_s.at[0], xf_r.at[0], pair_dev)]
    for i in range(1, 4):
        w_copies.append(w_send(i))

    xg[c, z] = x_ref[...]
    for ref, whole in weights:
        n = ref.shape[0]
        whole[pl.ds(pl.multiple_of(f * n, n), n), :] = ref[...]

    def w_forward(i):
        out = []
        for k in range(1, F):
            w_copies[i][k - 1].wait_recv()
            part = half_of(i, lax.rem(f + F - k, F), c)
            out.append(send(part, part, wf_s.at[i, k - 1], wf_r.at[i, k - 1], pair_dev))
        return out

    def x_forward(k):
        x_copies[k - 1].wait_recv()
        part = xg.at[c, lax.rem(z + H - k, H)]
        x_pair.append(send(part, part, xf_s.at[k], xf_r.at[k], pair_dev))

    for copy in w_forward(0):
        copy.wait_recv()
    g_all = lax.dot_general(
        dy_ref[...], wo_all[...], (((1,), (1,)), ((), ())), preferred_element_type=f32
    ).astype(bf)
    for h in range(H):
        g_send[h] = g_all[:, h * HD:(h + 1) * HD]
    g_copies = []
    for k in range(1, H):
        to = lax.rem(z + k, H)
        g_copies.append(send(g_send.at[to], g_got.at[z], g_s.at[k - 1], g_r.at[k - 1], head_dev(k)))
    g_got[z] = g_send[z]

    forwards = []
    forwards += w_forward(1)
    x_forward(1)
    forwards += w_forward(2)
    x_forward(3)
    x_forward(2)
    forwards += w_forward(3)
    for copy in forwards:
        copy.wait_recv()
    cols = pl.ds(pl.multiple_of(z * HD, HD), HD)
    wh[:, :HD] = wk_all[:, cols]
    wh[:, HD:2 * HD] = wv_all[:, cols]
    wh[:, 2 * HD:] = wq_all[:, cols]
    own_x = xg[c].reshape(H * rows, -1)
    own_kvq = dot_plain(own_x, wh[...]).astype(bf)
    kv_buf[c] = own_kvq[:, :2 * HD]
    for h in range(H):
        q_buf[h] = own_kvq[h * rows:(h + 1) * rows, 2 * HD:]
    for copy in x_pair:
        copy.wait_recv()
    kv_buf[other] = dot_plain(xg[other].reshape(H * rows, -1), wh[:, :2 * HD]).astype(bf)
    for copy in g_copies:
        copy.wait_recv()

    kv = kv_buf[...].reshape(2 * H * rows, 2 * HD)
    keys = kv[:, :HD]
    values = kv[:, HD:]
    spans = rows // SPAN
    at_copies, dq_copies = [], []
    for k in (1, 2, 3, 0):
        h = lax.rem(z + k, H)
        query = q_buf[h]
        grad = g_got[h]
        score = contract_cols(query, keys) * scale
        line = bias_ref[c, h]
        score = score + jnp.concatenate(
            [jnp.broadcast_to(line[s:s + 1], (SPAN, line.shape[1])) for s in range(spans)], axis=0
        )
        prob = jnp.exp(score - jnp.max(score, axis=1, keepdims=True))
        prob = prob * (1.0 / jnp.sum(prob, axis=1, keepdims=True))
        prob_b = prob.astype(bf)
        att = dot_plain(prob_b, values).astype(bf)
        att_send[h] = att
        if k == 0:
            att_own[:, cols] = att
        else:
            at_copies.append(send(
                att_send.at[h], att_own.at[:, cols], at_s.at[k - 1], at_r.at[k - 1], head_dev(k)
            ))
        d_prob = contract_cols(grad, values)
        delta = jnp.sum(prob * d_prob, axis=1, keepdims=True)
        d_score = (prob * (d_prob - delta) * scale).astype(bf)
        d_query = dot_plain(d_score, keys).astype(bf)
        dq_send[h] = d_query
        if k == 0:
            dq_own[:, cols] = d_query
        else:
            dq_copies.append(send(
                dq_send.at[h], dq_own.at[:, cols], dq_s.at[k - 1], dq_r.at[k - 1], head_dev(k)
            ))
        d_key = dot_rows(d_score, query).reshape(2, H * rows, HD)
        d_value = dot_rows(prob_b, grad).reshape(2, H * rows, HD)
        if k == 1:
            dkv_acc[:, :, :HD] = d_key
            dkv_acc[:, :, HD:] = d_value
        else:
            dkv_acc[:, :, :HD] += d_key
            dkv_acc[:, :, HD:] += d_value

    pair_dkv = send(dkv_acc.at[other], dkv_pair, pair_s.at[0], pair_r.at[0], pair_dev)

    for copy in at_copies:
        copy.wait_recv()
    attention = att_own[...]
    part = dot_rows(attention, dy_ref[...]).reshape(F, H, 2, -1, dy_ref.shape[1])
    for j in range(2):
        go0[j] = part[:, :, j].astype(bf)
    pair_go = send(go0.at[other], go0_got, pair_s.at[1], pair_r.at[1], pair_dev)

    pair_dkv.wait_recv()
    dkv = (dkv_acc[c] + dkv_pair[...]).astype(bf)
    for h in range(H):
        dkv_send[h] = dkv[h * rows:(h + 1) * rows]
        d_head[h * rows:(h + 1) * rows, :HD] = dq_send[h]
    d_head[:, HD:] = dkv
    dk_copies = []
    for k in range(1, H):
        to = lax.rem(z + k, H)
        dk_copies.append(send(
            dkv_send.at[to], dkv_own.at[z], dk_s.at[k - 1], dk_r.at[k - 1], head_dev(k)
        ))
    dkv_own[z] = dkv_send[z]

    part = dot_rows(xg[c].reshape(H * rows, -1), d_head[...]).reshape(F, H, 2, -1, 3 * HD)
    for j in range(2):
        gw0[j] = part[:, :, j].astype(bf)
    pair_gw = send(gw0.at[other], gw0_got, pair_s.at[2], pair_r.at[2], pair_dev)

    def over_clips(kept, got, out, slots, s, r):
        out[...] = (kept[c].astype(f32) + got[...].astype(f32)).astype(bf)
        return [
            send(out.at[lax.rem(f + k, F)], slots.at[k - 1], s.at[k - 1], r.at[k - 1], clip_dev(k))
            for k in range(1, F)
        ]

    def summed(copies, out, slots):
        total = out[f].astype(f32)
        for k in range(1, F):
            copies[k - 1].wait_recv()
            total = total + slots[k - 1].astype(f32)
        return total.astype(bf)

    pair_go.wait_recv()
    go_copies = over_clips(go0, go0_got, go1, go1_got, go1_s, go1_r)
    mixed_ref[...] = (x_ref[...].astype(f32) + dot_plain(attention, wo_all[...])).astype(bf)
    pair_gw.wait_recv()
    gw_copies = over_clips(gw0, gw0_got, gw1, gw1_got, gw1_s, gw1_r)

    for copy in dq_copies:
        copy.wait_recv()
    token = dy_ref[...].astype(f32) + contract_cols(dq_own[...], wq_all[...])
    for copy in dk_copies:
        copy.wait_recv()
    dk_rows = jnp.concatenate([dkv_own[h][:, :HD] for h in range(H)], axis=1)
    dv_rows = jnp.concatenate([dkv_own[h][:, HD:] for h in range(H)], axis=1)
    token = token + contract_cols(dk_rows, wk_all[...]) + contract_cols(dv_rows, wv_all[...])
    token_ref[...] = token.astype(bf)

    go2[...] = summed(go_copies, go1, go1_got)
    go_last = [
        send(go2.at[lax.rem(z + k, H)], go2_got.at[k - 1], go2_s.at[k - 1], go2_r.at[k - 1], head_dev(k))
        for k in range(1, H)
    ]
    gw2[...] = summed(gw_copies, gw1, gw1_got)
    gw_last = [
        send(gw2.at[lax.rem(z + k, H)], gw2_got.at[z], gw2_s.at[k - 1], gw2_r.at[k - 1], head_dev(k))
        for k in range(1, H)
    ]
    gw2_got[z] = gw2[z]
    total = go2[z].astype(f32)
    for k in range(1, H):
        go_last[k - 1].wait_recv()
        total = total + go2_got[k - 1].astype(f32)
    go_ref[...] = total
    for copy in gw_last:
        copy.wait_recv()
    for h in range(H):
        piece = gw2_got[h].astype(f32)
        gq_ref[:, h * HD:(h + 1) * HD] = piece[:, :HD]
        gk_ref[:, h * HD:(h + 1) * HD] = piece[:, HD:2 * HD]
        gv_ref[:, h * HD:(h + 1) * HD] = piece[:, 2 * HD:]
    for copy in started:
        copy.wait_send()


def fused_body(F, tokens, cotangent, w_query, w_key, w_value, w_out, block_mask, span_order):
    H = HEADS
    bf, f32 = jnp.bfloat16, jnp.float32
    x_rows, dy_rows = tokens[0], cotangent[0]
    rows, D = x_rows.shape
    HQ = w_query.shape[1]
    spans = rows // SPAN
    n_spans = span_order.shape[0]
    per_block = BLK // SPAN
    order = span_order.reshape(H, 2, spans).transpose(1, 0, 2).reshape(-1) // per_block
    hot = (order[:, None] == jnp.arange(block_mask.shape[0])[None, :]).astype(f32)
    linked = jnp.dot(jnp.dot(hot, (block_mask == 1).astype(f32)), hot.T)
    bias = jnp.where(linked > 0.5, 0.0, NEG).astype(f32)
    bias = jnp.broadcast_to(bias[:, :, None], (n_spans, n_spans, SPAN))
    bias = bias.reshape(2, H, spans, n_spans * SPAN)

    gq_rows = D // (F * H * 2)
    go_rows = HQ // (F * H * 2)
    V = pltpu.VMEM
    dma = pltpu.SemaphoreType.DMA
    hr = H * rows
    scratch = [
        V((2, H, rows, D), bf), V((D, HQ), bf), V((D, HQ), bf), V((D, HQ), bf), V((HQ, D), bf),
        V((D, 3 * HD), bf), V((H, rows, HD), bf), V((H, rows, HD), bf),
        V((2, hr, 2 * HD), bf), V((H, rows, HD), bf),
        V((H, rows, HD), bf), V((rows, HQ), bf), V((H, rows, HD), bf), V((rows, HQ), bf),
        V((2, hr, 2 * HD), f32), V((hr, 2 * HD), f32), V((H, rows, 2 * HD), bf),
        V((H, rows, 2 * HD), bf), V((hr, 3 * HD), bf),
        V((2, F, H, go_rows, D), bf), V((F, H, go_rows, D), bf), V((F, H, go_rows, D), bf),
        V((F - 1, H, go_rows, D), bf), V((H, go_rows, D), bf), V((H - 1, go_rows, D), bf),
        V((2, F, H, gq_rows, 3 * HD), bf), V((F, H, gq_rows, 3 * HD), bf),
        V((F, H, gq_rows, 3 * HD), bf), V((F - 1, H, gq_rows, 3 * HD), bf),
        V((H, gq_rows, 3 * HD), bf), V((H, gq_rows, 3 * HD), bf),
    ]
    for shape in (
        (H - 1,), (H,), (4, F - 1), (4, F - 1), (H - 1,), (H - 1,), (H - 1,), (H - 1,), (3,),
        (F - 1,), (H - 1,), (F - 1,), (H - 1,),
    ):
        scratch += [dma(shape), dma(shape)]
    mixed, token, gq, gk, gv, go = pl.pallas_call(
        functools.partial(fused_kernel, F),
        out_shape=(
            jax.ShapeDtypeStruct((rows, D), bf), jax.ShapeDtypeStruct((rows, D), bf),
            jax.ShapeDtypeStruct((gq_rows, HQ), f32), jax.ShapeDtypeStruct((gq_rows, HQ), f32),
            jax.ShapeDtypeStruct((gq_rows, HQ), f32), jax.ShapeDtypeStruct((go_rows, D), f32),
        ),
        in_specs=[pl.BlockSpec(memory_space=pltpu.VMEM)] * 7,
        out_specs=tuple([pl.BlockSpec(memory_space=pltpu.VMEM)] * 6),
        scratch_shapes=scratch,
        compiler_params=pltpu.CompilerParams(
            collective_id=0, has_side_effects=True, vmem_limit_bytes=48 * 1024 * 1024
        ),
        cost_estimate=pl.CostEstimate(
            flops=3 * 10**9, bytes_accessed=4 * 10**6, transcendentals=10**6
        ),
    )(x_rows, dy_rows, w_query, w_key, w_value, w_out, bias)
    return (mixed[None], token[None], gq, gk, gv, go)


def solution(mesh):
    shape = dict(mesh.shape)
    chosen = body
    if shape["ctx"] == 2 * HEADS and shape["fsdp"] == 4:
        chosen = functools.partial(fused_body, shape["fsdp"])
    return jax.shard_map(
        chosen,
        mesh=mesh,
        in_specs=(
            P("fsdp", "ctx", None),
            P("fsdp", "ctx", None),
            P("fsdp", None),
            P("fsdp", None),
            P("fsdp", None),
            P("fsdp", None),
            P(),
            P(),
        ),
        out_specs=(
            P("fsdp", "ctx", None),
            P("fsdp", "ctx", None),
            P(("fsdp", "ctx"), None),
            P(("fsdp", "ctx"), None),
            P(("fsdp", "ctx"), None),
            P(("fsdp", "ctx"), None),
        ),
        check_vma=False,
    )
```

```python
import functools
import math

import jax
import jax.numpy as jnp
from jax import lax
from jax.experimental import pallas as pl
from jax.experimental.pallas import tpu as pltpu
from jax.sharding import PartitionSpec as P

HEADS = 4
HD = 128
BLK = 128
SPAN = 64


NEG = -1e30
HIGH = lax.Precision.HIGHEST


def block_ids(span_order, start, count):
    rows = start + jnp.arange(count, dtype=jnp.int32)
    span = rows // SPAN
    lanes = jnp.arange(span_order.shape[0], dtype=jnp.int32)
    first = jnp.sum(jnp.where(span[:, None] == lanes[None, :], span_order[None, :], 0), axis=1)
    return (first * SPAN + rows % SPAN) // BLK


def allowed_between(mask_f, row_ids, col_ids):
    lanes = jnp.arange(mask_f.shape[0], dtype=jnp.int32)
    left = (row_ids[:, None] == lanes[None, :]).astype(jnp.float32)
    right = (col_ids[:, None] == lanes[None, :]).astype(jnp.float32)
    linked = jnp.dot(jnp.dot(left, mask_f), right.T)
    return linked > 0.5


def over_blocks(step, carry, pieces):
    count = pieces[0].shape[0]
    width = 512
    stacked = tuple((piece.reshape((count // width, width) + piece.shape[1:]) for piece in pieces))

    def scan_step(state, item):
        number, parts = item
        return (step(state, parts, number * width), None)

    numbers = jnp.arange(count // width, dtype=jnp.int32)
    carry, _ = lax.scan(scan_step, carry, (numbers, stacked))
    return carry


def contract_rows(left, right):
    return lax.dot_general(
        left, right, (((0,), (0,)), ((), ())), preferred_element_type=jnp.float32
    )


def contract_cols(left, right):
    return lax.dot_general(
        left, right, (((1,), (1,)), ((), ())), preferred_element_type=jnp.float32
    )


def body(tokens, cotangent, w_query, w_key, w_value, w_out, block_mask, span_order):
    x_rows = tokens[0]
    dy_rows = cotangent[0]
    rows = x_rows.shape[0]
    scale = 1.0 / math.sqrt(HD)
    full_q, full_k, full_v, full_o = (
        lax.all_gather(w_query, "fsdp", axis=0, tiled=True),
        lax.all_gather(w_key, "fsdp", axis=0, tiled=True),
        lax.all_gather(w_value, "fsdp", axis=0, tiled=True),
        lax.all_gather(w_out, "fsdp", axis=0, tiled=True),
    )
    query = jnp.dot(x_rows, full_q, preferred_element_type=jnp.float32).astype(jnp.bfloat16)
    keys = jnp.dot(x_rows, full_k, preferred_element_type=jnp.float32).astype(jnp.bfloat16)
    values = jnp.dot(x_rows, full_v, preferred_element_type=jnp.float32).astype(jnp.bfloat16)
    d_attn = contract_cols(dy_rows, full_o).astype(jnp.bfloat16)
    mask_f = block_mask.astype(jnp.float32)
    own_ids = block_ids(span_order, lax.axis_index("ctx") * rows, rows)
    q_own = query.reshape(rows, HEADS, HD)
    k_own = keys.reshape(rows, HEADS, HD)
    v_own = values.reshape(rows, HEADS, HD)
    g_own = d_attn.reshape(rows, HEADS, HD)

    def sweep_keys(carry, parts, start):
        top, total, out_acc, mix_acc, key_acc, dot_acc = carry
        count = parts[0].shape[0]
        k_part = parts[0].reshape(count, HEADS, HD)
        v_part = parts[1].reshape(count, HEADS, HD)
        keep = allowed_between(mask_f, own_ids, block_ids(span_order, start, count))[None]
        score = (
            jnp.einsum("qhd,khd->hqk", q_own, k_part, preferred_element_type=jnp.float32) * scale
        )
        score = jnp.where(keep, score, NEG)
        new_top = jnp.maximum(top, jnp.max(score, axis=-1))
        fade = jnp.exp(top - new_top)
        prob = jnp.where(keep, jnp.exp(score - new_top[:, :, None]), 0.0)
        k_wide = k_part.astype(jnp.float32)
        v_wide = v_part.astype(jnp.float32)
        total = fade * total + jnp.sum(prob, axis=-1)
        out_acc = fade[:, :, None] * out_acc + jnp.einsum(
            "hqk,khd->hqd", prob, v_wide, precision=HIGH
        )
        d_prob = jnp.einsum("qhd,khd->hqk", g_own, v_part, preferred_element_type=jnp.float32)
        weighted = prob * d_prob
        dot_acc = fade * dot_acc + jnp.sum(weighted, axis=-1)
        mix_acc = fade[:, :, None] * mix_acc + jnp.einsum(
            "hqk,khd->hqd", weighted, k_wide, precision=HIGH
        )
        key_acc = fade[:, :, None] * key_acc + jnp.einsum(
            "hqk,khd->hqd", prob, k_wide, precision=HIGH
        )
        return (new_top, total, out_acc, mix_acc, key_acc, dot_acc)

    flat = jnp.zeros((HEADS, rows), jnp.float32)
    cube = jnp.zeros((HEADS, rows, HD), jnp.float32)
    begin = (jnp.full((HEADS, rows), NEG, jnp.float32), flat, cube, cube, cube, flat)
    top, total, out_acc, mix_acc, key_acc, dot_acc = over_blocks(
        sweep_keys,
        begin,
        (
            lax.all_gather(keys, "ctx", axis=0, tiled=True),
            lax.all_gather(values, "ctx", axis=0, tiled=True),
        ),
    )
    share = 1.0 / total
    combined = out_acc * share[:, :, None]
    log_total = top + jnp.log(total)
    attention = jnp.transpose(combined, (1, 0, 2)).reshape(rows, HEADS * HD).astype(jnp.bfloat16)
    mixed = (
        x_rows.astype(jnp.float32) + jnp.dot(attention, full_o, preferred_element_type=jnp.float32)
    ).astype(jnp.bfloat16)
    delta = dot_acc * share
    log_rows = jnp.transpose(log_total)
    delta_rows = jnp.transpose(delta)

    def key_side(acc, parts, start):
        d_key, d_value = acc
        count = parts[0].shape[0]
        q_part = parts[0].reshape(count, HEADS, HD)
        g_part = parts[1].reshape(count, HEADS, HD)
        lse_part = jnp.transpose(parts[2])
        delta_part = jnp.transpose(parts[3])
        keep = allowed_between(mask_f, block_ids(span_order, start, count), own_ids)[None]
        score = (
            jnp.einsum("khd,qhd->hkq", q_part, k_own, preferred_element_type=jnp.float32) * scale
        )
        score = jnp.where(keep, score, NEG)
        prob = jnp.where(keep, jnp.exp(score - lse_part[:, :, None]), 0.0)
        d_prob = jnp.einsum("khd,qhd->hkq", g_part, v_own, preferred_element_type=jnp.float32)
        d_score = prob * (d_prob - delta_part[:, :, None])
        d_key = d_key + scale * jnp.einsum(
            "hkq,khd->hqd", d_score, q_part.astype(jnp.float32), precision=HIGH
        )
        d_value = d_value + jnp.einsum(
            "hkq,khd->hqd", prob, g_part.astype(jnp.float32), precision=HIGH
        )
        return (d_key, d_value)

    d_query = scale * (mix_acc - delta[:, :, None] * key_acc) * share[:, :, None]
    d_key, d_value = over_blocks(
        key_side,
        (cube, cube),
        (
            lax.all_gather(query.astype(jnp.float32), "ctx", axis=0, tiled=True).astype(
                jnp.bfloat16
            ),
            lax.all_gather(d_attn.astype(jnp.float32), "ctx", axis=0, tiled=True).astype(
                jnp.bfloat16
            ),
            lax.all_gather(log_rows, "ctx", axis=0, tiled=True),
            lax.all_gather(delta_rows, "ctx", axis=0, tiled=True),
        ),
    )

    def to_rows(grad_heads):
        return jnp.transpose(grad_heads, (1, 0, 2)).reshape(rows, HEADS * HD).astype(jnp.bfloat16)

    dq_rows = to_rows(d_query)
    dk_rows = to_rows(d_key)
    dv_rows = to_rows(d_value)
    token_grad = (
        dy_rows.astype(jnp.float32)
        + contract_cols(dq_rows, full_q)
        + contract_cols(dk_rows, full_k)
        + contract_cols(dv_rows, full_v)
    ).astype(jnp.bfloat16)
    grad_q = contract_rows(x_rows, dq_rows)
    grad_k = contract_rows(x_rows, dk_rows)
    grad_v = contract_rows(x_rows, dv_rows)
    grad_o = contract_rows(attention, dy_rows)
    grad_q, grad_k, grad_v, grad_o = (
        lax.psum_scatter(grad_q, ("fsdp", "ctx"), scatter_dimension=0, tiled=True),
        lax.psum_scatter(grad_k, ("fsdp", "ctx"), scatter_dimension=0, tiled=True),
        lax.psum_scatter(grad_v, ("fsdp", "ctx"), scatter_dimension=0, tiled=True),
        lax.psum_scatter(grad_o, ("fsdp", "ctx"), scatter_dimension=0, tiled=True),
    )
    return (mixed[None], token_grad[None], grad_q, grad_k, grad_v, grad_o)


def dot_rows(left, right):
    return lax.dot_general(
        left, right, (((0,), (0,)), ((), ())), preferred_element_type=jnp.float32
    )


def dot_plain(left, right):
    return jnp.dot(left, right, preferred_element_type=jnp.float32)


def fused_kernel(
    F,
    x_ref, dy_ref, wq_ref, wk_ref, wv_ref, wo_ref, mask_ref, order_ref,
    mixed_ref, token_ref, gq_ref, gk_ref, gv_ref, go_ref,
    xg, dy_own, wq_all, wk_all, wv_all, wo_all, wh, bias, g_send, g_got, kv_buf, q_buf,
    att_send, att_own, dq_send, dq_own, dkv_acc, dkv_pair, dkv_send, dkv_own, d_head,
    go0, go0_got, go1, go1_got, go2, go2_got,
    gw0, gw0_got, gw1, gw1_got, gw2, gw2_got,
    here, x_s, x_r, xf_s, xf_r, w_s, w_r, wf_s, wf_r, wh_s, wh_r, whf_s, whf_r,
    own_s, own_r, g_s, g_r, at_s, at_r, dq_s, dq_r,
    dk_s, dk_r, pair_s, pair_r, go1_s, go1_r, go2_s, go2_r, gw1_s, gw1_r, gw2_s, gw2_r,
):
    H = HEADS
    f = lax.axis_index("fsdp")
    ctx = lax.axis_index("ctx")
    z = ctx // 2
    c = ctx % 2
    other = 1 - c
    rows = x_ref.shape[0]
    bf = jnp.bfloat16
    f32 = jnp.float32
    scale = 1.0 / math.sqrt(HD)

    pair_dev = (f, z * 2 + other)

    def head_dev(k):
        return (f, lax.rem(z + k, H) * 2 + c)

    def clip_dev(k):
        return (lax.rem(f + k, F), ctx)

    started = []

    def remote(src, dst, s, r, dev):
        return pltpu.make_async_remote_copy(
            src_ref=src, dst_ref=dst, send_sem=s, recv_sem=r,
            device_id=dev, device_id_type=pl.DeviceIdType.MESH,
        )

    def send(src, dst, s, r, dev):
        copy = remote(src, dst, s, r, dev)
        copy.start()
        started.append(copy)
        return copy

    cols = pl.ds(pl.multiple_of(z * HD, HD), HD)
    weights = ((wo_ref, wo_all), (wk_ref, wk_all), (wv_ref, wv_all), (wq_ref, wq_all))
    heads = ((wk_ref, 0), (wv_ref, 1), (wq_ref, 2))

    def shard(i, owner):
        n = weights[i][0].shape[0]
        return weights[i][1].at[pl.ds(pl.multiple_of(owner * n, n), n)]

    shard_rows = wk_ref.shape[0]
    half_rows = shard_rows // 2

    def head_rows(i, owner, part):
        start = pl.multiple_of(owner * shard_rows + part * half_rows, half_rows)
        return wh.at[pl.ds(start, half_rows), pl.ds(i * HD, HD)]

    moves = [(x_ref, xg.at[c, z]), (dy_ref, dy_own)]
    moves += [(weights[i][0], shard(i, f)) for i in range(4)]
    moves += [
        (ref.at[:, cols], wh.at[pl.ds(pl.multiple_of(f * shard_rows, shard_rows), shard_rows), pl.ds(i * HD, HD)])
        for ref, i in heads
    ]
    local = [pltpu.make_async_copy(a, b, here.at[n]) for n, (a, b) in enumerate(moves)]
    for copy in local:
        copy.start()

    barrier = pltpu.get_barrier_semaphore()
    peers = [pair_dev] + [head_dev(k) for k in range(1, H)] + [clip_dev(k) for k in range(1, F)]
    for dev in peers:
        pl.semaphore_signal(barrier, inc=1, device_id=dev, device_id_type=pl.DeviceIdType.MESH)
    pl.semaphore_wait(barrier, len(peers))

    def flow(side, s):
        step = 1 if side == 0 else -1
        sent = z - step * s
        got = z - step * (s + 1)
        inside = (sent >= 0) & (sent <= H - 1)
        can_send = inside & (z < H - 1 if side == 0 else z > 0)
        can_recv = (got >= 0) & (got <= H - 1)
        src = x_ref if s == 0 else xg.at[c, sent]
        out = remote(src, xg.at[c, sent], x_s.at[side, s], x_r.at[side, s], (f, (z + step) * 2 + c))
        into = remote(src, xg.at[c, got], x_s.at[side, s], x_r.at[side, s], (f, (z + step) * 2 + c))
        part = xg.at[c, got]
        pair = remote(part, part, xf_s.at[side, s], xf_r.at[side, s], pair_dev)
        return can_send, can_recv, out, into, pair, got

    flows = {(side, s): flow(side, s) for s in range(H - 1) for side in range(2)}

    for side in range(2):
        can_send, _, out, _, _, _ = flows[side, 0]
        pl.when(can_send)(out.start)
    x_own = send(x_ref, xg.at[c, z], own_s.at[0], own_r.at[0], pair_dev)

    wh_copies = {}
    for ref, i in heads:
        src = ref.at[pl.ds(pl.multiple_of(c * half_rows, half_rows), half_rows), cols]
        for k in range(1, F):
            wh_copies[i, k] = send(
                src, head_rows(i, f, c), wh_s.at[i, k - 1], wh_r.at[i, k - 1], clip_dev(k)
            )

    def half_of(i, owner, part):
        n = weights[i][0].shape[0]
        start = pl.multiple_of(owner * n + part * (n // 2), n // 2)
        return weights[i][1].at[pl.ds(start, n // 2)]

    def w_send(i):
        ref = weights[i][0]
        n = ref.shape[0] // 2
        src = ref.at[pl.ds(pl.multiple_of(c * n, n), n)]
        return [
            send(src, half_of(i, f, c), w_s.at[i, k - 1], w_r.at[i, k - 1], clip_dev(k))
            for k in range(1, F)
        ]

    w_copies = {0: w_send(0)}

    def w_forward(i):
        out = []
        for k in range(1, F):
            w_copies[i][k - 1].wait_recv()
            part = half_of(i, lax.rem(f + F - k, F), c)
            out.append(send(part, part, wf_s.at[i, k - 1], wf_r.at[i, k - 1], pair_dev))
        return out

    spans = rows // SPAN
    per_block = BLK // SPAN
    width = bias.shape[1]
    place = lax.broadcasted_iota(jnp.int32, (1, width), 1) // SPAN
    key_block = [
        order_ref[(2 * h + j) * spans + s] // per_block
        for j in range(2) for h in range(H) for s in range(spans)
    ]
    for h in range(H):
        for s in range(spans):
            block = order_ref[(2 * h + c) * spans + s] // per_block
            line = jnp.full((1, width), NEG, f32)
            for n, key in enumerate(key_block):
                open_to = jnp.where(mask_ref[block, key] == 1, 0.0, NEG).astype(f32)
                line = jnp.where(place == n, open_to, line)
            bias[h * spans + s:h * spans + s + 1, :] = line

    for copy in local:
        copy.wait()

    forwards = []
    for k in range(1, F):
        for _, i in heads:
            wh_copies[i, k].wait_recv()
            part = head_rows(i, lax.rem(f + F - k, F), c)
            forwards.append(send(part, part, whf_s.at[i, k - 1], whf_r.at[i, k - 1], pair_dev))

    def pass_on(s):
        for side in range(2):
            _, can_recv, _, into, pair, _ = flows[side, s]

            @pl.when(can_recv)
            def _():
                into.wait_recv()
                pair.start()

            if s < H - 2:
                can_send, _, out, _, _, _ = flows[side, s + 1]
                pl.when(can_send)(out.start)

    def project_own(slot):
        out = dot_plain(xg[c, slot], wh[...]).astype(bf)
        kv_buf[c, slot] = out[:, :2 * HD]
        q_buf[slot] = out[:, 2 * HD:]

    def project_pair(slot):
        kv_buf[other, slot] = dot_plain(xg[other, slot], wh[:, :2 * HD]).astype(bf)

    def project(s):
        for side in range(2):
            _, can_recv, _, _, pair, got = flows[side, s]

            @pl.when(can_recv)
            def _():
                project_own(got)
                pair.wait_recv()
                project_pair(got)

    pass_on(0)
    wo_forwards = w_forward(0)
    for i in range(1, 4):
        w_copies[i] = w_send(i)
    for copy in forwards:
        copy.wait_recv()
    project_own(z)
    x_own.wait_recv()
    project_pair(z)
    pass_on(1)
    for copy in wo_forwards:
        copy.wait_recv()
    g_all = contract_cols(dy_own[...], wo_all[...]).astype(bf)
    for h in range(H):
        g_send[h] = g_all[:, h * HD:(h + 1) * HD]
    g_copies = []
    for k in range(1, H):
        to = lax.rem(z + k, H)
        g_copies.append(send(g_send.at[to], g_got.at[z], g_s.at[k - 1], g_r.at[k - 1], head_dev(k)))
    g_got[z] = g_send[z]
    project(0)
    project(1)
    pass_on(2)
    project(2)
    for copy in g_copies:
        copy.wait_recv()

    kv = kv_buf[...].reshape(2 * H * rows, 2 * HD)
    keys = kv[:, :HD]
    values = kv[:, HD:]
    at_copies, dq_copies = [], []
    late = []
    for k in (1, 2, 3, 0):
        h = lax.rem(z + k, H)
        query = q_buf[h]
        grad = g_got[h]
        score = contract_cols(query, keys) * scale
        score = score + jnp.concatenate(
            [
                jnp.broadcast_to(bias[pl.ds(h * spans + s, 1), :], (SPAN, width))
                for s in range(spans)
            ],
            axis=0,
        )
        prob = jnp.exp(score - jnp.max(score, axis=1, keepdims=True))
        prob = prob * (1.0 / jnp.sum(prob, axis=1, keepdims=True))
        prob_b = prob.astype(bf)
        att = dot_plain(prob_b, values).astype(bf)
        att_send[h] = att
        if k == 0:
            att_own[:, cols] = att
        else:
            at_copies.append(send(
                att_send.at[h], att_own.at[:, cols], at_s.at[k - 1], at_r.at[k - 1], head_dev(k)
            ))
        d_prob = contract_cols(grad, values)
        delta = jnp.sum(prob * d_prob, axis=1, keepdims=True)
        d_score = (prob * (d_prob - delta) * scale).astype(bf)
        d_query = dot_plain(d_score, keys).astype(bf)
        dq_send[h] = d_query
        if k == 0:
            dq_own[:, cols] = d_query
        else:
            dq_copies.append(send(
                dq_send.at[h], dq_own.at[:, cols], dq_s.at[k - 1], dq_r.at[k - 1], head_dev(k)
            ))
        d_key = dot_rows(d_score, query).reshape(2, H * rows, HD)
        d_value = dot_rows(prob_b, grad).reshape(2, H * rows, HD)
        if k == 1:
            dkv_acc[:, :, :HD] = d_key
            dkv_acc[:, :, HD:] = d_value
        else:
            dkv_acc[:, :, :HD] += d_key
            dkv_acc[:, :, HD:] += d_value

    for i in (3, 1, 2):
        late += w_forward(i)
    pair_dkv = send(dkv_acc.at[other], dkv_pair, pair_s.at[0], pair_r.at[0], pair_dev)

    for copy in at_copies:
        copy.wait_recv()
    attention = att_own[...]
    part = dot_rows(attention, dy_own[...]).reshape(F, H, 2, -1, dy_own.shape[1])
    for j in range(2):
        go0[j] = part[:, :, j].astype(bf)
    pair_go = send(go0.at[other], go0_got, pair_s.at[1], pair_r.at[1], pair_dev)

    pair_dkv.wait_recv()
    dkv = (dkv_acc[c] + dkv_pair[...]).astype(bf)
    for h in range(H):
        dkv_send[h] = dkv[h * rows:(h + 1) * rows]
        d_head[h * rows:(h + 1) * rows, :HD] = dq_send[h]
    d_head[:, HD:] = dkv
    dk_copies = []
    for k in range(1, H):
        to = lax.rem(z + k, H)
        dk_copies.append(send(
            dkv_send.at[to], dkv_own.at[z], dk_s.at[k - 1], dk_r.at[k - 1], head_dev(k)
        ))
    dkv_own[z] = dkv_send[z]

    part = dot_rows(xg[c].reshape(H * rows, -1), d_head[...]).reshape(F, H, 2, -1, 3 * HD)
    for j in range(2):
        gw0[j] = part[:, :, j].astype(bf)
    pair_gw = send(gw0.at[other], gw0_got, pair_s.at[2], pair_r.at[2], pair_dev)

    def over_clips(kept, got, out, slots, s, r):
        out[...] = (kept[c].astype(f32) + got[...].astype(f32)).astype(bf)
        return [
            send(out.at[lax.rem(f + k, F)], slots.at[k - 1], s.at[k - 1], r.at[k - 1], clip_dev(k))
            for k in range(1, F)
        ]

    def summed(copies, out, slots):
        total = out[f].astype(f32)
        for k in range(1, F):
            copies[k - 1].wait_recv()
            total = total + slots[k - 1].astype(f32)
        return total.astype(bf)

    pair_go.wait_recv()
    go_copies = over_clips(go0, go0_got, go1, go1_got, go1_s, go1_r)
    mixed_ref[...] = (xg[c, z].astype(f32) + dot_plain(attention, wo_all[...])).astype(bf)
    pair_gw.wait_recv()
    gw_copies = over_clips(gw0, gw0_got, gw1, gw1_got, gw1_s, gw1_r)

    for copy in dq_copies:
        copy.wait_recv()
    for copy in late:
        copy.wait_recv()
    token = dy_own[...].astype(f32) + contract_cols(dq_own[...], wq_all[...])
    for copy in dk_copies:
        copy.wait_recv()
    dk_rows = jnp.concatenate([dkv_own[h][:, :HD] for h in range(H)], axis=1)
    dv_rows = jnp.concatenate([dkv_own[h][:, HD:] for h in range(H)], axis=1)
    token = token + contract_cols(dk_rows, wk_all[...]) + contract_cols(dv_rows, wv_all[...])
    token_ref[...] = token.astype(bf)

    go2[...] = summed(go_copies, go1, go1_got)
    go_last = [
        send(go2.at[lax.rem(z + k, H)], go2_got.at[k - 1], go2_s.at[k - 1], go2_r.at[k - 1], head_dev(k))
        for k in range(1, H)
    ]
    gw2[...] = summed(gw_copies, gw1, gw1_got)
    gw_last = [
        send(gw2.at[lax.rem(z + k, H)], gw2_got.at[z], gw2_s.at[k - 1], gw2_r.at[k - 1], head_dev(k))
        for k in range(1, H)
    ]
    gw2_got[z] = gw2[z]
    total = go2[z].astype(f32)
    for k in range(1, H):
        go_last[k - 1].wait_recv()
        total = total + go2_got[k - 1].astype(f32)
    go_ref[...] = total
    for copy in gw_last:
        copy.wait_recv()
    for h in range(H):
        piece = gw2_got[h].astype(f32)
        gq_ref[:, h * HD:(h + 1) * HD] = piece[:, :HD]
        gk_ref[:, h * HD:(h + 1) * HD] = piece[:, HD:2 * HD]
        gv_ref[:, h * HD:(h + 1) * HD] = piece[:, 2 * HD:]
    for copy in started:
        copy.wait_send()
    for can_send, can_recv, out, _, pair, _ in flows.values():
        pl.when(can_send)(out.wait_send)
        pl.when(can_recv)(pair.wait_send)


def store_kernel(*refs):
    n = (len(refs) - 1) // 2
    sems = refs[-1]
    copies = [pltpu.make_async_copy(refs[i], refs[n + i], sems.at[i]) for i in range(n)]
    for copy in copies:
        copy.start()
    for copy in copies:
        copy.wait()


def fused_body(F, tokens, cotangent, w_query, w_key, w_value, w_out, block_mask, span_order):
    H = HEADS
    bf, f32 = jnp.bfloat16, jnp.float32
    x_rows, dy_rows = tokens[0], cotangent[0]
    rows, D = x_rows.shape
    HQ = w_query.shape[1]
    gq_rows = D // (F * H * 2)
    go_rows = HQ // (F * H * 2)
    V = pltpu.VMEM
    dma = pltpu.SemaphoreType.DMA
    hr = H * rows
    scratch = [
        V((2, H, rows, D), bf), V((rows, D), bf), V((D, HQ), bf), V((D, HQ), bf), V((D, HQ), bf), V((HQ, D), bf),
        V((D, 3 * HD), bf), V((hr // SPAN, 2 * hr), f32), V((H, rows, HD), bf), V((H, rows, HD), bf),
        V((2, H, rows, 2 * HD), bf), V((H, rows, HD), bf),
        V((H, rows, HD), bf), V((rows, HQ), bf), V((H, rows, HD), bf), V((rows, HQ), bf),
        V((2, hr, 2 * HD), f32), V((hr, 2 * HD), f32), V((H, rows, 2 * HD), bf),
        V((H, rows, 2 * HD), bf), V((hr, 3 * HD), bf),
        V((2, F, H, go_rows, D), bf), V((F, H, go_rows, D), bf), V((F, H, go_rows, D), bf),
        V((F - 1, H, go_rows, D), bf), V((H, go_rows, D), bf), V((H - 1, go_rows, D), bf),
        V((2, F, H, gq_rows, 3 * HD), bf), V((F, H, gq_rows, 3 * HD), bf),
        V((F, H, gq_rows, 3 * HD), bf), V((F - 1, H, gq_rows, 3 * HD), bf),
        V((H, gq_rows, 3 * HD), bf), V((H, gq_rows, 3 * HD), bf),
    ]
    scratch.append(dma((9,)))
    for shape in (
        (2, H - 1), (2, H - 1), (4, F - 1), (4, F - 1), (3, F - 1), (3, F - 1), (1,), (H - 1,), (H - 1,), (H - 1,), (H - 1,), (3,),
        (F - 1,), (H - 1,), (F - 1,), (H - 1,),
    ):
        scratch += [dma(shape), dma(shape)]
    vmem = pl.BlockSpec(memory_space=pltpu.VMEM)
    smem = pl.BlockSpec(memory_space=pltpu.SMEM)
    results = pl.pallas_call(
        functools.partial(fused_kernel, F),
        out_shape=(
            jax.ShapeDtypeStruct((rows, D), bf), jax.ShapeDtypeStruct((rows, D), bf),
            jax.ShapeDtypeStruct((gq_rows, HQ), f32), jax.ShapeDtypeStruct((gq_rows, HQ), f32),
            jax.ShapeDtypeStruct((gq_rows, HQ), f32), jax.ShapeDtypeStruct((go_rows, D), f32),
        ),
        in_specs=[pl.BlockSpec(memory_space=pltpu.HBM)] * 6 + [smem] * 2,
        out_specs=tuple([vmem] * 6),
        scratch_shapes=scratch,
        compiler_params=pltpu.CompilerParams(
            collective_id=0, has_side_effects=True, vmem_limit_bytes=60 * 1024 * 1024
        ),
        cost_estimate=pl.CostEstimate(
            flops=3 * 10**9, bytes_accessed=4 * 10**6, transcendentals=10**6
        ),
    )(x_rows, dy_rows, w_query, w_key, w_value, w_out, block_mask, span_order)
    mixed, token, gq, gk, gv, go = pl.pallas_call(
        store_kernel,
        out_shape=tuple(jax.ShapeDtypeStruct(r.shape, r.dtype) for r in results),
        in_specs=[pl.BlockSpec(memory_space=pltpu.HBM)] * 6,
        out_specs=tuple([pl.BlockSpec(memory_space=pltpu.HBM)] * 6),
        scratch_shapes=[dma((6,))],
        compiler_params=pltpu.CompilerParams(vmem_limit_bytes=60 * 1024 * 1024),
    )(*results)
    return (mixed[None], token[None], gq, gk, gv, go)


def solution(mesh):
    shape = dict(mesh.shape)
    chosen = body
    if shape["ctx"] == 2 * HEADS and shape["fsdp"] == 4:
        chosen = functools.partial(fused_body, shape["fsdp"])
    return jax.shard_map(
        chosen,
        mesh=mesh,
        in_specs=(
            P("fsdp", "ctx", None),
            P("fsdp", "ctx", None),
            P("fsdp", None),
            P("fsdp", None),
            P("fsdp", None),
            P("fsdp", None),
            P(),
            P(),
        ),
        out_specs=(
            P("fsdp", "ctx", None),
            P("fsdp", "ctx", None),
            P(("fsdp", "ctx"), None),
            P(("fsdp", "ctx"), None),
            P(("fsdp", "ctx"), None),
            P(("fsdp", "ctx"), None),
        ),
        check_vma=False,
    )
```

```python
import functools
import math

import jax
import jax.numpy as jnp
from jax import lax
from jax.experimental import pallas as pl
from jax.experimental.pallas import tpu as pltpu
from jax.sharding import PartitionSpec as P

HEADS = 4
HD = 128
BLK = 128
SPAN = 64


NEG = -1e30
HIGH = lax.Precision.HIGHEST


def block_ids(span_order, start, count):
    rows = start + jnp.arange(count, dtype=jnp.int32)
    span = rows // SPAN
    lanes = jnp.arange(span_order.shape[0], dtype=jnp.int32)
    first = jnp.sum(jnp.where(span[:, None] == lanes[None, :], span_order[None, :], 0), axis=1)
    return (first * SPAN + rows % SPAN) // BLK


def allowed_between(mask_f, row_ids, col_ids):
    lanes = jnp.arange(mask_f.shape[0], dtype=jnp.int32)
    left = (row_ids[:, None] == lanes[None, :]).astype(jnp.float32)
    right = (col_ids[:, None] == lanes[None, :]).astype(jnp.float32)
    linked = jnp.dot(jnp.dot(left, mask_f), right.T)
    return linked > 0.5


def over_blocks(step, carry, pieces):
    count = pieces[0].shape[0]
    width = 512
    stacked = tuple((piece.reshape((count // width, width) + piece.shape[1:]) for piece in pieces))

    def scan_step(state, item):
        number, parts = item
        return (step(state, parts, number * width), None)

    numbers = jnp.arange(count // width, dtype=jnp.int32)
    carry, _ = lax.scan(scan_step, carry, (numbers, stacked))
    return carry


def contract_rows(left, right):
    return lax.dot_general(
        left, right, (((0,), (0,)), ((), ())), preferred_element_type=jnp.float32
    )


def contract_cols(left, right):
    return lax.dot_general(
        left, right, (((1,), (1,)), ((), ())), preferred_element_type=jnp.float32
    )


def body(tokens, cotangent, w_query, w_key, w_value, w_out, block_mask, span_order):
    x_rows = tokens[0]
    dy_rows = cotangent[0]
    rows = x_rows.shape[0]
    scale = 1.0 / math.sqrt(HD)
    full_q, full_k, full_v, full_o = (
        lax.all_gather(w_query, "fsdp", axis=0, tiled=True),
        lax.all_gather(w_key, "fsdp", axis=0, tiled=True),
        lax.all_gather(w_value, "fsdp", axis=0, tiled=True),
        lax.all_gather(w_out, "fsdp", axis=0, tiled=True),
    )
    query = jnp.dot(x_rows, full_q, preferred_element_type=jnp.float32).astype(jnp.bfloat16)
    keys = jnp.dot(x_rows, full_k, preferred_element_type=jnp.float32).astype(jnp.bfloat16)
    values = jnp.dot(x_rows, full_v, preferred_element_type=jnp.float32).astype(jnp.bfloat16)
    d_attn = contract_cols(dy_rows, full_o).astype(jnp.bfloat16)
    mask_f = block_mask.astype(jnp.float32)
    own_ids = block_ids(span_order, lax.axis_index("ctx") * rows, rows)
    q_own = query.reshape(rows, HEADS, HD)
    k_own = keys.reshape(rows, HEADS, HD)
    v_own = values.reshape(rows, HEADS, HD)
    g_own = d_attn.reshape(rows, HEADS, HD)

    def sweep_keys(carry, parts, start):
        top, total, out_acc, mix_acc, key_acc, dot_acc = carry
        count = parts[0].shape[0]
        k_part = parts[0].reshape(count, HEADS, HD)
        v_part = parts[1].reshape(count, HEADS, HD)
        keep = allowed_between(mask_f, own_ids, block_ids(span_order, start, count))[None]
        score = (
            jnp.einsum("qhd,khd->hqk", q_own, k_part, preferred_element_type=jnp.float32) * scale
        )
        score = jnp.where(keep, score, NEG)
        new_top = jnp.maximum(top, jnp.max(score, axis=-1))
        fade = jnp.exp(top - new_top)
        prob = jnp.where(keep, jnp.exp(score - new_top[:, :, None]), 0.0)
        k_wide = k_part.astype(jnp.float32)
        v_wide = v_part.astype(jnp.float32)
        total = fade * total + jnp.sum(prob, axis=-1)
        out_acc = fade[:, :, None] * out_acc + jnp.einsum(
            "hqk,khd->hqd", prob, v_wide, precision=HIGH
        )
        d_prob = jnp.einsum("qhd,khd->hqk", g_own, v_part, preferred_element_type=jnp.float32)
        weighted = prob * d_prob
        dot_acc = fade * dot_acc + jnp.sum(weighted, axis=-1)
        mix_acc = fade[:, :, None] * mix_acc + jnp.einsum(
            "hqk,khd->hqd", weighted, k_wide, precision=HIGH
        )
        key_acc = fade[:, :, None] * key_acc + jnp.einsum(
            "hqk,khd->hqd", prob, k_wide, precision=HIGH
        )
        return (new_top, total, out_acc, mix_acc, key_acc, dot_acc)

    flat = jnp.zeros((HEADS, rows), jnp.float32)
    cube = jnp.zeros((HEADS, rows, HD), jnp.float32)
    begin = (jnp.full((HEADS, rows), NEG, jnp.float32), flat, cube, cube, cube, flat)
    top, total, out_acc, mix_acc, key_acc, dot_acc = over_blocks(
        sweep_keys,
        begin,
        (
            lax.all_gather(keys, "ctx", axis=0, tiled=True),
            lax.all_gather(values, "ctx", axis=0, tiled=True),
        ),
    )
    share = 1.0 / total
    combined = out_acc * share[:, :, None]
    log_total = top + jnp.log(total)
    attention = jnp.transpose(combined, (1, 0, 2)).reshape(rows, HEADS * HD).astype(jnp.bfloat16)
    mixed = (
        x_rows.astype(jnp.float32) + jnp.dot(attention, full_o, preferred_element_type=jnp.float32)
    ).astype(jnp.bfloat16)
    delta = dot_acc * share
    log_rows = jnp.transpose(log_total)
    delta_rows = jnp.transpose(delta)

    def key_side(acc, parts, start):
        d_key, d_value = acc
        count = parts[0].shape[0]
        q_part = parts[0].reshape(count, HEADS, HD)
        g_part = parts[1].reshape(count, HEADS, HD)
        lse_part = jnp.transpose(parts[2])
        delta_part = jnp.transpose(parts[3])
        keep = allowed_between(mask_f, block_ids(span_order, start, count), own_ids)[None]
        score = (
            jnp.einsum("khd,qhd->hkq", q_part, k_own, preferred_element_type=jnp.float32) * scale
        )
        score = jnp.where(keep, score, NEG)
        prob = jnp.where(keep, jnp.exp(score - lse_part[:, :, None]), 0.0)
        d_prob = jnp.einsum("khd,qhd->hkq", g_part, v_own, preferred_element_type=jnp.float32)
        d_score = prob * (d_prob - delta_part[:, :, None])
        d_key = d_key + scale * jnp.einsum(
            "hkq,khd->hqd", d_score, q_part.astype(jnp.float32), precision=HIGH
        )
        d_value = d_value + jnp.einsum(
            "hkq,khd->hqd", prob, g_part.astype(jnp.float32), precision=HIGH
        )
        return (d_key, d_value)

    d_query = scale * (mix_acc - delta[:, :, None] * key_acc) * share[:, :, None]
    d_key, d_value = over_blocks(
        key_side,
        (cube, cube),
        (
            lax.all_gather(query.astype(jnp.float32), "ctx", axis=0, tiled=True).astype(
                jnp.bfloat16
            ),
            lax.all_gather(d_attn.astype(jnp.float32), "ctx", axis=0, tiled=True).astype(
                jnp.bfloat16
            ),
            lax.all_gather(log_rows, "ctx", axis=0, tiled=True),
            lax.all_gather(delta_rows, "ctx", axis=0, tiled=True),
        ),
    )

    def to_rows(grad_heads):
        return jnp.transpose(grad_heads, (1, 0, 2)).reshape(rows, HEADS * HD).astype(jnp.bfloat16)

    dq_rows = to_rows(d_query)
    dk_rows = to_rows(d_key)
    dv_rows = to_rows(d_value)
    token_grad = (
        dy_rows.astype(jnp.float32)
        + contract_cols(dq_rows, full_q)
        + contract_cols(dk_rows, full_k)
        + contract_cols(dv_rows, full_v)
    ).astype(jnp.bfloat16)
    grad_q = contract_rows(x_rows, dq_rows)
    grad_k = contract_rows(x_rows, dk_rows)
    grad_v = contract_rows(x_rows, dv_rows)
    grad_o = contract_rows(attention, dy_rows)
    grad_q, grad_k, grad_v, grad_o = (
        lax.psum_scatter(grad_q, ("fsdp", "ctx"), scatter_dimension=0, tiled=True),
        lax.psum_scatter(grad_k, ("fsdp", "ctx"), scatter_dimension=0, tiled=True),
        lax.psum_scatter(grad_v, ("fsdp", "ctx"), scatter_dimension=0, tiled=True),
        lax.psum_scatter(grad_o, ("fsdp", "ctx"), scatter_dimension=0, tiled=True),
    )
    return (mixed[None], token_grad[None], grad_q, grad_k, grad_v, grad_o)


def dot_rows(left, right):
    return lax.dot_general(
        left, right, (((0,), (0,)), ((), ())), preferred_element_type=jnp.float32
    )


def dot_plain(left, right):
    return jnp.dot(left, right, preferred_element_type=jnp.float32)


def fused_kernel(
    F,
    x_ref, dy_ref, wq_ref, wk_ref, wv_ref, wo_ref, mask_ref, order_ref,
    mixed_ref, token_ref, gq_ref, gk_ref, gv_ref, go_ref,
    xg, dy_own, wq_all, wk_all, wv_all, wo_all, wh, bias, g_send, g_got, kv_buf, q_buf,
    att_send, att_own, dq_send, dq_own, dk_send, dk_own, dv_send, dv_own,
    p_buf, dk_acc, dk_pair, dv_acc, dv_pair, xt,
    go0, go0_got, go1, go1_got, go2, go2_got,
    gv0, gv0_got, gv1, gv1_got, gv2, gv2_got,
    gw0, gw0_got, gw1, gw1_got, gw2, gw2_got,
    here, x_s, x_r, xf_s, xf_r, w_s, w_r, wf_s, wf_r, wh_s, wh_r, whf_s, whf_r,
    own_s, own_r, g_s, g_r, at_s, at_r, dq_s, dq_r,
    dk_s, dk_r, dv_s, dv_r, pair_s, pair_r, go1_s, go1_r, go2_s, go2_r,
    gv1_s, gv1_r, gv2_s, gv2_r, gw1_s, gw1_r, gw2_s, gw2_r,
):
    H = HEADS
    f = lax.axis_index("fsdp")
    ctx = lax.axis_index("ctx")
    z = ctx // 2
    c = ctx % 2
    other = 1 - c
    rows = x_ref.shape[0]
    bf = jnp.bfloat16
    f32 = jnp.float32
    scale = 1.0 / math.sqrt(HD)

    pair_dev = (f, z * 2 + other)

    def head_dev(k):
        return (f, lax.rem(z + k, H) * 2 + c)

    def clip_dev(k):
        return (lax.rem(f + k, F), ctx)

    started = []

    def remote(src, dst, s, r, dev):
        return pltpu.make_async_remote_copy(
            src_ref=src, dst_ref=dst, send_sem=s, recv_sem=r,
            device_id=dev, device_id_type=pl.DeviceIdType.MESH,
        )

    def send(src, dst, s, r, dev):
        copy = remote(src, dst, s, r, dev)
        copy.start()
        started.append(copy)
        return copy

    cols = pl.ds(pl.multiple_of(z * HD, HD), HD)
    weights = ((wo_ref, wo_all), (wk_ref, wk_all), (wv_ref, wv_all), (wq_ref, wq_all))
    heads = ((wk_ref, 0), (wv_ref, 1), (wq_ref, 2))

    def shard(i, owner):
        n = weights[i][0].shape[0]
        return weights[i][1].at[pl.ds(pl.multiple_of(owner * n, n), n)]

    shard_rows = wk_ref.shape[0]
    half_rows = shard_rows // 2

    def head_rows(i, owner, part):
        start = pl.multiple_of(owner * shard_rows + part * half_rows, half_rows)
        return wh.at[pl.ds(start, half_rows), pl.ds(i * HD, HD)]

    moves = [(x_ref, xg.at[c, z]), (dy_ref, dy_own)]
    moves += [(weights[i][0], shard(i, f)) for i in range(4)]
    moves += [
        (ref.at[:, cols], wh.at[pl.ds(pl.multiple_of(f * shard_rows, shard_rows), shard_rows), pl.ds(i * HD, HD)])
        for ref, i in heads
    ]
    local = [pltpu.make_async_copy(a, b, here.at[n]) for n, (a, b) in enumerate(moves)]
    for copy in local:
        copy.start()

    barrier = pltpu.get_barrier_semaphore()
    peers = [pair_dev] + [head_dev(k) for k in range(1, H)] + [clip_dev(k) for k in range(1, F)]
    for dev in peers:
        pl.semaphore_signal(barrier, inc=1, device_id=dev, device_id_type=pl.DeviceIdType.MESH)
    pl.semaphore_wait(barrier, len(peers))

    def flow(side, s):
        step = 1 if side == 0 else -1
        sent = z - step * s
        got = z - step * (s + 1)
        inside = (sent >= 0) & (sent <= H - 1)
        can_send = inside & (z < H - 1 if side == 0 else z > 0)
        can_recv = (got >= 0) & (got <= H - 1)
        src = x_ref if s == 0 else xg.at[c, sent]
        out = remote(src, xg.at[c, sent], x_s.at[side, s], x_r.at[side, s], (f, (z + step) * 2 + c))
        into = remote(src, xg.at[c, got], x_s.at[side, s], x_r.at[side, s], (f, (z + step) * 2 + c))
        part = xg.at[c, got]
        pair = remote(part, part, xf_s.at[side, s], xf_r.at[side, s], pair_dev)
        return can_send, can_recv, out, into, pair, got

    flows = {(side, s): flow(side, s) for s in range(H - 1) for side in range(2)}

    for side in range(2):
        can_send, _, out, _, _, _ = flows[side, 0]
        pl.when(can_send)(out.start)
    x_own = send(x_ref, xg.at[c, z], own_s.at[0], own_r.at[0], pair_dev)

    wh_copies = {}
    for ref, i in heads:
        src = ref.at[pl.ds(pl.multiple_of(c * half_rows, half_rows), half_rows), cols]
        for k in range(1, F):
            wh_copies[i, k] = send(
                src, head_rows(i, f, c), wh_s.at[i, k - 1], wh_r.at[i, k - 1], clip_dev(k)
            )

    def half_of(i, owner, part):
        n = weights[i][0].shape[0]
        start = pl.multiple_of(owner * n + part * (n // 2), n // 2)
        return weights[i][1].at[pl.ds(start, n // 2)]

    def w_send(i):
        ref = weights[i][0]
        n = ref.shape[0] // 2
        src = ref.at[pl.ds(pl.multiple_of(c * n, n), n)]
        return [
            send(src, half_of(i, f, c), w_s.at[i, k - 1], w_r.at[i, k - 1], clip_dev(k))
            for k in range(1, F)
        ]

    w_copies = {0: w_send(0)}

    def w_forward(i):
        out = []
        for k in range(1, F):
            w_copies[i][k - 1].wait_recv()
            part = half_of(i, lax.rem(f + F - k, F), c)
            out.append(send(part, part, wf_s.at[i, k - 1], wf_r.at[i, k - 1], pair_dev))
        return out

    spans = rows // SPAN
    per_block = BLK // SPAN
    width = bias.shape[1]
    place = lax.broadcasted_iota(jnp.int32, (1, width), 1) // SPAN
    key_block = [
        order_ref[(2 * h + j) * spans + s] // per_block
        for j in range(2) for h in range(H) for s in range(spans)
    ]
    for h in range(H):
        for s in range(spans):
            block = order_ref[(2 * h + c) * spans + s] // per_block
            line = jnp.full((1, width), NEG, f32)
            for n, key in enumerate(key_block):
                open_to = jnp.where(mask_ref[block, key] == 1, 0.0, NEG).astype(f32)
                line = jnp.where(place == n, open_to, line)
            bias[h * spans + s:h * spans + s + 1, :] = line

    for copy in local:
        copy.wait()

    forwards = []
    for k in range(1, F):
        for _, i in heads:
            wh_copies[i, k].wait_recv()
            part = head_rows(i, lax.rem(f + F - k, F), c)
            forwards.append(send(part, part, whf_s.at[i, k - 1], whf_r.at[i, k - 1], pair_dev))

    def pass_on(s):
        for side in range(2):
            _, can_recv, _, into, pair, _ = flows[side, s]

            @pl.when(can_recv)
            def _():
                into.wait_recv()
                pair.start()

            if s < H - 2:
                can_send, _, out, _, _, _ = flows[side, s + 1]
                pl.when(can_send)(out.start)

    def project_own(slot):
        out = dot_plain(xg[c, slot], wh[...]).astype(bf)
        kv_buf[c, slot] = out[:, :2 * HD]
        q_buf[slot] = out[:, 2 * HD:]
        xt[:, pl.ds(pl.multiple_of(slot * rows, rows), rows)] = xg[c, slot].T

    def project_pair(slot):
        kv_buf[other, slot] = dot_plain(xg[other, slot], wh[:, :2 * HD]).astype(bf)

    def project(s):
        for side in range(2):
            _, can_recv, _, _, pair, got = flows[side, s]

            @pl.when(can_recv)
            def _():
                project_own(got)
                pair.wait_recv()
                project_pair(got)

    pass_on(0)
    wo_forwards = w_forward(0)
    for i in range(1, 4):
        w_copies[i] = w_send(i)
    for copy in forwards:
        copy.wait_recv()
    project_own(z)
    x_own.wait_recv()
    project_pair(z)
    pass_on(1)
    for copy in wo_forwards:
        copy.wait_recv()
    g_all = contract_cols(dy_own[...], wo_all[...]).astype(bf)
    for h in range(H):
        g_send[h] = g_all[:, h * HD:(h + 1) * HD]
    g_copies = []
    for k in range(1, H):
        to = lax.rem(z + k, H)
        g_copies.append(send(g_send.at[to], g_got.at[z], g_s.at[k - 1], g_r.at[k - 1], head_dev(k)))
    g_got[z] = g_send[z]
    project(0)
    project(1)
    pass_on(2)
    project(2)
    for copy in g_copies:
        copy.wait_recv()

    kv = kv_buf[...].reshape(2 * H * rows, 2 * HD)
    keys = kv[:, :HD]
    values = kv[:, HD:]
    blocks = ((1, 2), (3, 0))

    def slots_of(ks):
        return [lax.rem(z + k, H) for k in ks]

    def stacked(buf, ks):
        return jnp.concatenate([buf[h] for h in slots_of(ks)], axis=0)

    def deal(value, ks, slots, own, s, r):
        out = []
        for n, (k, h) in enumerate(zip(ks, slots_of(ks))):
            piece = value[n * rows:(n + 1) * rows]
            slots[h] = piece
            if k == 0:
                own[:, cols] = piece
            else:
                out.append(send(slots.at[h], own.at[:, cols], s.at[k - 1], r.at[k - 1], head_dev(k)))
        return out

    def halves(ref, value, n):
        value = value.reshape(2, H * rows, HD)
        ref[...] = value if n == 0 else ref[...] + value

    at_copies = []
    for n, ks in enumerate(blocks):
        score = contract_cols(stacked(q_buf, ks), keys) * scale
        score = score + jnp.concatenate(
            [
                jnp.broadcast_to(bias[pl.ds(h * spans + s, 1), :], (SPAN, width))
                for h in slots_of(ks) for s in range(spans)
            ],
            axis=0,
        )
        prob = jnp.exp(score - jnp.max(score, axis=1, keepdims=True))
        prob = prob * (1.0 / jnp.sum(prob, axis=1, keepdims=True))
        p_buf[n] = prob
        prob_b = prob.astype(bf)
        at_copies += deal(dot_plain(prob_b, values).astype(bf), ks, att_send, att_own, at_s, at_r)
        halves(dv_acc, dot_rows(prob_b, stacked(g_got, ks)), n)
    pair_dv = send(dv_acc.at[other], dv_pair, pair_s.at[0], pair_r.at[0], pair_dev)

    dq_copies = []

    def backward(n):
        ks = blocks[n]
        d_prob = contract_cols(stacked(g_got, ks), values)
        prob = p_buf[n]
        delta = jnp.sum(prob * d_prob, axis=1, keepdims=True)
        d_score = (prob * (d_prob - delta) * scale).astype(bf)
        d_query = dot_plain(d_score, keys).astype(bf)
        halves(dk_acc, dot_rows(d_score, stacked(q_buf, ks)), n)
        return deal(d_query, ks, dq_send, dq_own, dq_s, dq_r)

    def finish(acc, pair, copy, slots, own, s, r):
        copy.wait_recv()
        total = (acc[c] + pair[...]).astype(bf)
        for h in range(H):
            slots[h] = total[h * rows:(h + 1) * rows]
        own[:, cols] = slots[z]
        return total, [
            send(
                slots.at[lax.rem(z + k, H)], own.at[:, cols], s.at[k - 1], r.at[k - 1], head_dev(k)
            )
            for k in range(1, H)
        ]

    def split(ref, value, at=None):
        value = value.reshape(F, H, 2, -1, value.shape[1])
        for j in range(2):
            if at is None:
                ref[j] = value[:, :, j].astype(bf)
            else:
                ref[j, :, :, :, at * HD:(at + 1) * HD] = value[:, :, j].astype(bf)

    def over_clips(kept, got, out, slots, s, r):
        out[...] = (kept[c].astype(f32) + got[...].astype(f32)).astype(bf)
        return [
            send(out.at[lax.rem(f + k, F)], slots.at[k - 1], s.at[k - 1], r.at[k - 1], clip_dev(k))
            for k in range(1, F)
        ]

    def summed(copies, out, slots):
        total = out[f].astype(f32)
        for k in range(1, F):
            copies[k - 1].wait_recv()
            total = total + slots[k - 1].astype(f32)
        return total.astype(bf)

    dq_copies += backward(0)
    for copy in at_copies:
        copy.wait_recv()
    attention = att_own[...]
    split(go0, dot_rows(attention, dy_own[...]))
    pair_go = send(go0.at[other], go0_got, pair_s.at[1], pair_r.at[1], pair_dev)
    d_value, dv_copies = finish(dv_acc, dv_pair, pair_dv, dv_send, dv_own, dv_s, dv_r)
    late = []
    for i in (1, 2, 3):
        late += w_forward(i)
    dq_copies += backward(1)
    pair_dk = send(dk_acc.at[other], dk_pair, pair_s.at[2], pair_r.at[2], pair_dev)

    split(gv0, dot_plain(xt[...], d_value))
    pair_gv = send(gv0.at[other], gv0_got, pair_s.at[3], pair_r.at[3], pair_dev)
    pair_go.wait_recv()
    go_copies = over_clips(go0, go0_got, go1, go1_got, go1_s, go1_r)
    split(gw0, dot_plain(xt[...], dq_send[...].reshape(H * rows, HD)), 0)
    d_key, dk_copies = finish(dk_acc, dk_pair, pair_dk, dk_send, dk_own, dk_s, dk_r)
    split(gw0, dot_plain(xt[...], d_key), 1)
    pair_gw = send(gw0.at[other], gw0_got, pair_s.at[4], pair_r.at[4], pair_dev)
    pair_gv.wait_recv()
    gv_copies = over_clips(gv0, gv0_got, gv1, gv1_got, gv1_s, gv1_r)
    mixed_ref[...] = (xg[c, z].astype(f32) + dot_plain(attention, wo_all[...])).astype(bf)
    pair_gw.wait_recv()
    gw_copies = over_clips(gw0, gw0_got, gw1, gw1_got, gw1_s, gw1_r)

    for copy in late + dv_copies + dq_copies:
        copy.wait_recv()
    token = dy_own[...].astype(f32) + contract_cols(dv_own[...], wv_all[...])
    token = token + contract_cols(dq_own[...], wq_all[...])
    for copy in dk_copies:
        copy.wait_recv()
    token_ref[...] = (token + contract_cols(dk_own[...], wk_all[...])).astype(bf)

    def to_owner(ref, got, s, r):
        got[z] = ref[z]
        return [
            send(ref.at[lax.rem(z + k, H)], got.at[z], s.at[k - 1], r.at[k - 1], head_dev(k))
            for k in range(1, H)
        ]

    go2[...] = summed(go_copies, go1, go1_got)
    last = to_owner(go2, go2_got, go2_s, go2_r)
    gv2[...] = summed(gv_copies, gv1, gv1_got)
    last += to_owner(gv2, gv2_got, gv2_s, gv2_r)
    gw2[...] = summed(gw_copies, gw1, gw1_got)
    last += to_owner(gw2, gw2_got, gw2_s, gw2_r)
    for copy in last:
        copy.wait_recv()
    total = go2_got[0].astype(f32)
    for h in range(1, H):
        total = total + go2_got[h].astype(f32)
    go_ref[...] = total
    for h in range(H):
        piece = gw2_got[h].astype(f32)
        gq_ref[:, h * HD:(h + 1) * HD] = piece[:, :HD]
        gk_ref[:, h * HD:(h + 1) * HD] = piece[:, HD:]
        gv_ref[:, h * HD:(h + 1) * HD] = gv2_got[h].astype(f32)
    for copy in started:
        copy.wait_send()
    for can_send, can_recv, out, _, pair, _ in flows.values():
        pl.when(can_send)(out.wait_send)
        pl.when(can_recv)(pair.wait_send)


def store_kernel(*refs):
    n = (len(refs) - 2) // 3
    srcs, outs, held = refs[:n], refs[n:2 * n], refs[2 * n:3 * n]
    sems_in, sems_out = refs[-2:]
    loads = [pltpu.make_async_copy(srcs[i], held[i], sems_in.at[i]) for i in range(n)]
    stores = [pltpu.make_async_copy(held[i], outs[i], sems_out.at[i]) for i in range(n)]
    for load in loads:
        load.start()
    for load, store in zip(loads, stores):
        load.wait()
        store.start()
    for store in stores:
        store.wait()


def fused_body(F, tokens, cotangent, w_query, w_key, w_value, w_out, block_mask, span_order):
    H = HEADS
    bf, f32 = jnp.bfloat16, jnp.float32
    x_rows, dy_rows = tokens[0], cotangent[0]
    rows, D = x_rows.shape
    HQ = w_query.shape[1]
    gq_rows = D // (F * H * 2)
    go_rows = HQ // (F * H * 2)
    V = pltpu.VMEM
    dma = pltpu.SemaphoreType.DMA
    hr = H * rows
    scratch = [
        V((2, H, rows, D), bf), V((rows, D), bf), V((D, HQ), bf), V((D, HQ), bf), V((D, HQ), bf), V((HQ, D), bf),
        V((D, 3 * HD), bf), V((hr // SPAN, 2 * hr), f32), V((H, rows, HD), bf), V((H, rows, HD), bf),
        V((2, H, rows, 2 * HD), bf), V((H, rows, HD), bf),
    ]
    for _ in range(4):
        scratch += [V((H, rows, HD), bf), V((rows, HQ), bf)]
    scratch.append(V((2, hr // 2, 2 * hr), f32))
    for _ in range(2):
        scratch += [V((2, hr, HD), f32), V((hr, HD), f32)]
    scratch.append(V((D, hr), bf))
    for n, wide in ((go_rows, D), (gq_rows, HD), (gq_rows, 2 * HD)):
        scratch += [
            V((2, F, H, n, wide), bf), V((F, H, n, wide), bf), V((F, H, n, wide), bf),
            V((F - 1, H, n, wide), bf), V((H, n, wide), bf), V((H, n, wide), bf),
        ]
    scratch.append(dma((9,)))
    head, clip = (H - 1,), (F - 1,)
    for shape in (
        (2, H - 1), (2, H - 1), (4, F - 1), (4, F - 1), (3, F - 1), (3, F - 1), (1,),
        head, head, head, head, head, (5,), clip, head, clip, head, clip, head,
    ):
        scratch += [dma(shape), dma(shape)]
    vmem = pl.BlockSpec(memory_space=pltpu.VMEM)
    smem = pl.BlockSpec(memory_space=pltpu.SMEM)
    results = pl.pallas_call(
        functools.partial(fused_kernel, F),
        out_shape=(
            jax.ShapeDtypeStruct((rows, D), bf), jax.ShapeDtypeStruct((rows, D), bf),
            jax.ShapeDtypeStruct((gq_rows, HQ), f32), jax.ShapeDtypeStruct((gq_rows, HQ), f32),
            jax.ShapeDtypeStruct((gq_rows, HQ), f32), jax.ShapeDtypeStruct((go_rows, D), f32),
        ),
        in_specs=[pl.BlockSpec(memory_space=pltpu.HBM)] * 6 + [smem] * 2,
        out_specs=tuple([vmem] * 6),
        scratch_shapes=scratch,
        compiler_params=pltpu.CompilerParams(
            collective_id=0, has_side_effects=True, vmem_limit_bytes=60 * 1024 * 1024
        ),
        cost_estimate=pl.CostEstimate(
            flops=3 * 10**9, bytes_accessed=4 * 10**6, transcendentals=10**6
        ),
    )(x_rows, dy_rows, w_query, w_key, w_value, w_out, block_mask, span_order)
    mixed, token, gq, gk, gv, go = pl.pallas_call(
        store_kernel,
        out_shape=tuple(jax.ShapeDtypeStruct(r.shape, r.dtype) for r in results),
        in_specs=[pl.BlockSpec(memory_space=pltpu.HBM)] * 6,
        out_specs=tuple([pl.BlockSpec(memory_space=pltpu.HBM)] * 6),
        scratch_shapes=[V(r.shape, r.dtype) for r in results] + [dma((6,)), dma((6,))],
        compiler_params=pltpu.CompilerParams(vmem_limit_bytes=60 * 1024 * 1024),
    )(*results)
    return (mixed[None], token[None], gq, gk, gv, go)


def solution(mesh):
    shape = dict(mesh.shape)
    chosen = body
    if shape["ctx"] == 2 * HEADS and shape["fsdp"] == 4:
        chosen = functools.partial(fused_body, shape["fsdp"])
    return jax.shard_map(
        chosen,
        mesh=mesh,
        in_specs=(
            P("fsdp", "ctx", None),
            P("fsdp", "ctx", None),
            P("fsdp", None),
            P("fsdp", None),
            P("fsdp", None),
            P("fsdp", None),
            P(),
            P(),
        ),
        out_specs=(
            P("fsdp", "ctx", None),
            P("fsdp", "ctx", None),
            P(("fsdp", "ctx"), None),
            P(("fsdp", "ctx"), None),
            P(("fsdp", "ctx"), None),
            P(("fsdp", "ctx"), None),
        ),
        check_vma=False,
    )
```

```python
import functools
import math

import jax
import jax.numpy as jnp
from jax import lax
from jax.experimental import pallas as pl
from jax.experimental.pallas import tpu as pltpu
from jax.sharding import PartitionSpec as P

HEADS = 4
HD = 128
BLK = 128
SPAN = 64


NEG = -1e30
HIGH = lax.Precision.HIGHEST


def block_ids(span_order, start, count):
    rows = start + jnp.arange(count, dtype=jnp.int32)
    span = rows // SPAN
    lanes = jnp.arange(span_order.shape[0], dtype=jnp.int32)
    first = jnp.sum(jnp.where(span[:, None] == lanes[None, :], span_order[None, :], 0), axis=1)
    return (first * SPAN + rows % SPAN) // BLK


def allowed_between(mask_f, row_ids, col_ids):
    lanes = jnp.arange(mask_f.shape[0], dtype=jnp.int32)
    left = (row_ids[:, None] == lanes[None, :]).astype(jnp.float32)
    right = (col_ids[:, None] == lanes[None, :]).astype(jnp.float32)
    linked = jnp.dot(jnp.dot(left, mask_f), right.T)
    return linked > 0.5


def over_blocks(step, carry, pieces):
    count = pieces[0].shape[0]
    width = 512
    stacked = tuple((piece.reshape((count // width, width) + piece.shape[1:]) for piece in pieces))

    def scan_step(state, item):
        number, parts = item
        return (step(state, parts, number * width), None)

    numbers = jnp.arange(count // width, dtype=jnp.int32)
    carry, _ = lax.scan(scan_step, carry, (numbers, stacked))
    return carry


def contract_rows(left, right):
    return lax.dot_general(
        left, right, (((0,), (0,)), ((), ())), preferred_element_type=jnp.float32
    )


def contract_cols(left, right):
    return lax.dot_general(
        left, right, (((1,), (1,)), ((), ())), preferred_element_type=jnp.float32
    )


def body(tokens, cotangent, w_query, w_key, w_value, w_out, block_mask, span_order):
    x_rows = tokens[0]
    dy_rows = cotangent[0]
    rows = x_rows.shape[0]
    scale = 1.0 / math.sqrt(HD)
    full_q, full_k, full_v, full_o = (
        lax.all_gather(w_query, "fsdp", axis=0, tiled=True),
        lax.all_gather(w_key, "fsdp", axis=0, tiled=True),
        lax.all_gather(w_value, "fsdp", axis=0, tiled=True),
        lax.all_gather(w_out, "fsdp", axis=0, tiled=True),
    )
    query = jnp.dot(x_rows, full_q, preferred_element_type=jnp.float32).astype(jnp.bfloat16)
    keys = jnp.dot(x_rows, full_k, preferred_element_type=jnp.float32).astype(jnp.bfloat16)
    values = jnp.dot(x_rows, full_v, preferred_element_type=jnp.float32).astype(jnp.bfloat16)
    d_attn = contract_cols(dy_rows, full_o).astype(jnp.bfloat16)
    mask_f = block_mask.astype(jnp.float32)
    own_ids = block_ids(span_order, lax.axis_index("ctx") * rows, rows)
    q_own = query.reshape(rows, HEADS, HD)
    k_own = keys.reshape(rows, HEADS, HD)
    v_own = values.reshape(rows, HEADS, HD)
    g_own = d_attn.reshape(rows, HEADS, HD)

    def sweep_keys(carry, parts, start):
        top, total, out_acc, mix_acc, key_acc, dot_acc = carry
        count = parts[0].shape[0]
        k_part = parts[0].reshape(count, HEADS, HD)
        v_part = parts[1].reshape(count, HEADS, HD)
        keep = allowed_between(mask_f, own_ids, block_ids(span_order, start, count))[None]
        score = (
            jnp.einsum("qhd,khd->hqk", q_own, k_part, preferred_element_type=jnp.float32) * scale
        )
        score = jnp.where(keep, score, NEG)
        new_top = jnp.maximum(top, jnp.max(score, axis=-1))
        fade = jnp.exp(top - new_top)
        prob = jnp.where(keep, jnp.exp(score - new_top[:, :, None]), 0.0)
        k_wide = k_part.astype(jnp.float32)
        v_wide = v_part.astype(jnp.float32)
        total = fade * total + jnp.sum(prob, axis=-1)
        out_acc = fade[:, :, None] * out_acc + jnp.einsum(
            "hqk,khd->hqd", prob, v_wide, precision=HIGH
        )
        d_prob = jnp.einsum("qhd,khd->hqk", g_own, v_part, preferred_element_type=jnp.float32)
        weighted = prob * d_prob
        dot_acc = fade * dot_acc + jnp.sum(weighted, axis=-1)
        mix_acc = fade[:, :, None] * mix_acc + jnp.einsum(
            "hqk,khd->hqd", weighted, k_wide, precision=HIGH
        )
        key_acc = fade[:, :, None] * key_acc + jnp.einsum(
            "hqk,khd->hqd", prob, k_wide, precision=HIGH
        )
        return (new_top, total, out_acc, mix_acc, key_acc, dot_acc)

    flat = jnp.zeros((HEADS, rows), jnp.float32)
    cube = jnp.zeros((HEADS, rows, HD), jnp.float32)
    begin = (jnp.full((HEADS, rows), NEG, jnp.float32), flat, cube, cube, cube, flat)
    top, total, out_acc, mix_acc, key_acc, dot_acc = over_blocks(
        sweep_keys,
        begin,
        (
            lax.all_gather(keys, "ctx", axis=0, tiled=True),
            lax.all_gather(values, "ctx", axis=0, tiled=True),
        ),
    )
    share = 1.0 / total
    combined = out_acc * share[:, :, None]
    log_total = top + jnp.log(total)
    attention = jnp.transpose(combined, (1, 0, 2)).reshape(rows, HEADS * HD).astype(jnp.bfloat16)
    mixed = (
        x_rows.astype(jnp.float32) + jnp.dot(attention, full_o, preferred_element_type=jnp.float32)
    ).astype(jnp.bfloat16)
    delta = dot_acc * share
    log_rows = jnp.transpose(log_total)
    delta_rows = jnp.transpose(delta)

    def key_side(acc, parts, start):
        d_key, d_value = acc
        count = parts[0].shape[0]
        q_part = parts[0].reshape(count, HEADS, HD)
        g_part = parts[1].reshape(count, HEADS, HD)
        lse_part = jnp.transpose(parts[2])
        delta_part = jnp.transpose(parts[3])
        keep = allowed_between(mask_f, block_ids(span_order, start, count), own_ids)[None]
        score = (
            jnp.einsum("khd,qhd->hkq", q_part, k_own, preferred_element_type=jnp.float32) * scale
        )
        score = jnp.where(keep, score, NEG)
        prob = jnp.where(keep, jnp.exp(score - lse_part[:, :, None]), 0.0)
        d_prob = jnp.einsum("khd,qhd->hkq", g_part, v_own, preferred_element_type=jnp.float32)
        d_score = prob * (d_prob - delta_part[:, :, None])
        d_key = d_key + scale * jnp.einsum(
            "hkq,khd->hqd", d_score, q_part.astype(jnp.float32), precision=HIGH
        )
        d_value = d_value + jnp.einsum(
            "hkq,khd->hqd", prob, g_part.astype(jnp.float32), precision=HIGH
        )
        return (d_key, d_value)

    d_query = scale * (mix_acc - delta[:, :, None] * key_acc) * share[:, :, None]
    d_key, d_value = over_blocks(
        key_side,
        (cube, cube),
        (
            lax.all_gather(query.astype(jnp.float32), "ctx", axis=0, tiled=True).astype(
                jnp.bfloat16
            ),
            lax.all_gather(d_attn.astype(jnp.float32), "ctx", axis=0, tiled=True).astype(
                jnp.bfloat16
            ),
            lax.all_gather(log_rows, "ctx", axis=0, tiled=True),
            lax.all_gather(delta_rows, "ctx", axis=0, tiled=True),
        ),
    )

    def to_rows(grad_heads):
        return jnp.transpose(grad_heads, (1, 0, 2)).reshape(rows, HEADS * HD).astype(jnp.bfloat16)

    dq_rows = to_rows(d_query)
    dk_rows = to_rows(d_key)
    dv_rows = to_rows(d_value)
    token_grad = (
        dy_rows.astype(jnp.float32)
        + contract_cols(dq_rows, full_q)
        + contract_cols(dk_rows, full_k)
        + contract_cols(dv_rows, full_v)
    ).astype(jnp.bfloat16)
    grad_q = contract_rows(x_rows, dq_rows)
    grad_k = contract_rows(x_rows, dk_rows)
    grad_v = contract_rows(x_rows, dv_rows)
    grad_o = contract_rows(attention, dy_rows)
    grad_q, grad_k, grad_v, grad_o = (
        lax.psum_scatter(grad_q, ("fsdp", "ctx"), scatter_dimension=0, tiled=True),
        lax.psum_scatter(grad_k, ("fsdp", "ctx"), scatter_dimension=0, tiled=True),
        lax.psum_scatter(grad_v, ("fsdp", "ctx"), scatter_dimension=0, tiled=True),
        lax.psum_scatter(grad_o, ("fsdp", "ctx"), scatter_dimension=0, tiled=True),
    )
    return (mixed[None], token_grad[None], grad_q, grad_k, grad_v, grad_o)


def dot_rows(left, right):
    return lax.dot_general(
        left, right, (((0,), (0,)), ((), ())), preferred_element_type=jnp.float32
    )


def dot_plain(left, right):
    return jnp.dot(left, right, preferred_element_type=jnp.float32)


def fused_kernel(
    F,
    x_ref, dy_ref, wq_ref, wk_ref, wv_ref, wo_ref, mask_ref, order_ref,
    mixed_ref, token_ref, gq_ref, gk_ref, gv_ref, go_ref,
    xg, dy_own, wq_all, wk_all, wv_all, wo_all, wh, bias, g_send, g_got, kv_buf, q_buf,
    att_send, att_own, dq_send, dq_own, dk_send, dk_own, dv_send, dv_own,
    p_buf, s_buf, b_buf, dk_acc, dk_pair, dv_acc, dv_pair, xt,
    go0, go0_got, go1, go1_got, go2, go2_got,
    gv0, gv0_got, gv1, gv1_got, gv2, gv2_got,
    gw0, gw0_got, gw1, gw1_got, gw2, gw2_got,
    here, x_s, x_r, xf_s, xf_r, w_s, w_r, wf_s, wf_r, wh_s, wh_r, whf_s, whf_r,
    own_s, own_r, g_s, g_r, at_s, at_r, dq_s, dq_r,
    dk_s, dk_r, dv_s, dv_r, pair_s, pair_r, go1_s, go1_r, go2_s, go2_r,
    gv1_s, gv1_r, gv2_s, gv2_r, gw1_s, gw1_r, gw2_s, gw2_r,
):
    H = HEADS
    f = lax.axis_index("fsdp")
    ctx = lax.axis_index("ctx")
    z = ctx // 2
    c = ctx % 2
    other = 1 - c
    rows = x_ref.shape[0]
    bf = jnp.bfloat16
    f32 = jnp.float32
    scale = 1.0 / math.sqrt(HD)

    pair_dev = (f, z * 2 + other)

    def head_dev(k):
        return (f, lax.rem(z + k, H) * 2 + c)

    def clip_dev(k):
        return (lax.rem(f + k, F), ctx)

    started = []

    def remote(src, dst, s, r, dev):
        return pltpu.make_async_remote_copy(
            src_ref=src, dst_ref=dst, send_sem=s, recv_sem=r,
            device_id=dev, device_id_type=pl.DeviceIdType.MESH,
        )

    def send(src, dst, s, r, dev):
        copy = remote(src, dst, s, r, dev)
        copy.start()
        started.append(copy)
        return copy

    cols = pl.ds(pl.multiple_of(z * HD, HD), HD)
    weights = ((wo_ref, wo_all), (wk_ref, wk_all), (wv_ref, wv_all), (wq_ref, wq_all))
    heads = ((wk_ref, 0), (wv_ref, 1), (wq_ref, 2))

    def shard(i, owner):
        n = weights[i][0].shape[0]
        return weights[i][1].at[pl.ds(pl.multiple_of(owner * n, n), n)]

    shard_rows = wk_ref.shape[0]
    half_rows = shard_rows // 2

    def head_rows(i, owner, part):
        start = pl.multiple_of(owner * shard_rows + part * half_rows, half_rows)
        return wh.at[pl.ds(start, half_rows), pl.ds(i * HD, HD)]

    moves = [(x_ref, xg.at[c, z]), (dy_ref, dy_own)]
    moves += [(weights[i][0], shard(i, f)) for i in range(4)]
    moves += [
        (ref.at[:, cols], wh.at[pl.ds(pl.multiple_of(f * shard_rows, shard_rows), shard_rows), pl.ds(i * HD, HD)])
        for ref, i in heads
    ]
    local = [pltpu.make_async_copy(a, b, here.at[n]) for n, (a, b) in enumerate(moves)]
    for copy in local:
        copy.start()

    barrier = pltpu.get_barrier_semaphore()
    peers = [pair_dev] + [head_dev(k) for k in range(1, H)] + [clip_dev(k) for k in range(1, F)]
    for dev in peers:
        pl.semaphore_signal(barrier, inc=1, device_id=dev, device_id_type=pl.DeviceIdType.MESH)
    pl.semaphore_wait(barrier, len(peers))

    def flow(side, s):
        step = 1 if side == 0 else -1
        sent = z - step * s
        got = z - step * (s + 1)
        inside = (sent >= 0) & (sent <= H - 1)
        can_send = inside & (z < H - 1 if side == 0 else z > 0)
        can_recv = (got >= 0) & (got <= H - 1)
        src = x_ref if s == 0 else xg.at[c, sent]
        out = remote(src, xg.at[c, sent], x_s.at[side, s], x_r.at[side, s], (f, (z + step) * 2 + c))
        into = remote(src, xg.at[c, got], x_s.at[side, s], x_r.at[side, s], (f, (z + step) * 2 + c))
        part = xg.at[c, got]
        pair = remote(part, part, xf_s.at[side, s], xf_r.at[side, s], pair_dev)
        return can_send, can_recv, out, into, pair, got

    flows = {(side, s): flow(side, s) for s in range(H - 1) for side in range(2)}

    for side in range(2):
        can_send, _, out, _, _, _ = flows[side, 0]
        pl.when(can_send)(out.start)
    x_own = send(x_ref, xg.at[c, z], own_s.at[0], own_r.at[0], pair_dev)

    wh_copies = {}
    for ref, i in heads:
        src = ref.at[pl.ds(pl.multiple_of(c * half_rows, half_rows), half_rows), cols]
        for k in range(1, F):
            wh_copies[i, k] = send(
                src, head_rows(i, f, c), wh_s.at[i, k - 1], wh_r.at[i, k - 1], clip_dev(k)
            )

    def half_of(i, owner, part):
        n = weights[i][0].shape[0]
        start = pl.multiple_of(owner * n + part * (n // 2), n // 2)
        return weights[i][1].at[pl.ds(start, n // 2)]

    def w_send(i):
        ref = weights[i][0]
        n = ref.shape[0] // 2
        src = ref.at[pl.ds(pl.multiple_of(c * n, n), n)]
        return [
            send(src, half_of(i, f, c), w_s.at[i, k - 1], w_r.at[i, k - 1], clip_dev(k))
            for k in range(1, F)
        ]

    w_copies = {0: w_send(0)}

    def w_forward(i):
        out = []
        for k in range(1, F):
            w_copies[i][k - 1].wait_recv()
            part = half_of(i, lax.rem(f + F - k, F), c)
            out.append(send(part, part, wf_s.at[i, k - 1], wf_r.at[i, k - 1], pair_dev))
        return out

    spans = rows // SPAN
    per_block = BLK // SPAN
    width = bias.shape[1]
    place = lax.broadcasted_iota(jnp.int32, (1, width), 1) // SPAN
    key_block = [
        order_ref[(2 * h + j) * spans + s] // per_block
        for j in range(2) for h in range(H) for s in range(spans)
    ]
    for h in range(H):
        for s in range(spans):
            block = order_ref[(2 * h + c) * spans + s] // per_block
            line = jnp.full((1, width), NEG, f32)
            for n, key in enumerate(key_block):
                open_to = jnp.where(mask_ref[block, key] == 1, 0.0, NEG).astype(f32)
                line = jnp.where(place == n, open_to, line)
            bias[h * spans + s:h * spans + s + 1, :] = line

    for copy in local:
        copy.wait()

    forwards = []
    for k in range(1, F):
        for _, i in heads:
            wh_copies[i, k].wait_recv()
            part = head_rows(i, lax.rem(f + F - k, F), c)
            forwards.append(send(part, part, whf_s.at[i, k - 1], whf_r.at[i, k - 1], pair_dev))

    def pass_on(s):
        for side in range(2):
            _, can_recv, _, into, pair, _ = flows[side, s]

            @pl.when(can_recv)
            def _():
                into.wait_recv()
                pair.start()

            if s < H - 2:
                can_send, _, out, _, _, _ = flows[side, s + 1]
                pl.when(can_send)(out.start)

    def project_own(slot):
        out = dot_plain(xg[c, slot], wh[...]).astype(bf)
        kv_buf[c, slot] = out[:, :2 * HD]
        q_buf[slot] = out[:, 2 * HD:]
        xt[:, pl.ds(pl.multiple_of(slot * rows, rows), rows)] = xg[c, slot].T

    def project_pair(slot):
        kv_buf[other, slot] = dot_plain(xg[other, slot], wh[:, :2 * HD]).astype(bf)

    def project(s):
        for side in range(2):
            _, can_recv, _, _, pair, got = flows[side, s]

            @pl.when(can_recv)
            def _():
                project_own(got)
                pair.wait_recv()
                project_pair(got)

    pass_on(0)
    wo_forwards = w_forward(0)
    for i in (2, 3, 1):
        w_copies[i] = w_send(i)
    for copy in forwards:
        copy.wait_recv()
    project_own(z)
    x_own.wait_recv()
    project_pair(z)
    pass_on(1)
    for copy in wo_forwards:
        copy.wait_recv()
    g_all = contract_cols(dy_own[...], wo_all[...]).astype(bf)
    for h in range(H):
        g_send[h] = g_all[:, h * HD:(h + 1) * HD]
    g_copies = []
    for k in range(1, H):
        to = lax.rem(z + k, H)
        g_copies.append(send(g_send.at[to], g_got.at[z], g_s.at[k - 1], g_r.at[k - 1], head_dev(k)))
    g_got[z] = g_send[z]
    project(0)
    project(1)
    pass_on(2)
    project(2)
    for copy in g_copies:
        copy.wait_recv()

    kv = kv_buf[...].reshape(2 * H * rows, 2 * HD)
    keys = kv[:, :HD]
    values = kv[:, HD:]
    blocks = ((1, 2), (3, 0))

    def slots_of(ks):
        return [lax.rem(z + k, H) for k in ks]

    def stacked(buf, ks):
        return jnp.concatenate([buf[h] for h in slots_of(ks)], axis=0)

    def deal(value, ks, slots, own, s, r):
        out = []
        for n, (k, h) in enumerate(zip(ks, slots_of(ks))):
            piece = value[n * rows:(n + 1) * rows]
            slots[h] = piece
            if k == 0:
                own[:, cols] = piece
            else:
                out.append(send(slots.at[h], own.at[:, cols], s.at[k - 1], r.at[k - 1], head_dev(k)))
        return out

    def halves(ref, value, n):
        value = value.reshape(2, H * rows, HD)
        ref[...] = value if n == 0 else ref[...] + value

    at_copies = []
    for n, ks in enumerate(blocks):
        s_buf[...] = contract_cols(stacked(q_buf, ks), keys)
        lines = [bias[pl.ds(h * spans + s, 1), :] for h in slots_of(ks) for s in range(spans)]
        for start in range(0, s_buf.shape[0], 16):
            now = slice(start, start + 16)
            score = s_buf[now, :] * scale + lines[start // SPAN]
            prob = jnp.exp(score - jnp.max(score, axis=1, keepdims=True))
            prob = prob * (1.0 / jnp.sum(prob, axis=1, keepdims=True))
            p_buf[n, now, :] = prob
            b_buf[now, :] = prob.astype(bf)
        prob_b = b_buf[...]
        at_copies += deal(dot_plain(prob_b, values).astype(bf), ks, att_send, att_own, at_s, at_r)
        halves(dv_acc, dot_rows(prob_b, stacked(g_got, ks)), n)
    pair_dv = send(dv_acc.at[other], dv_pair, pair_s.at[0], pair_r.at[0], pair_dev)

    dq_copies = []

    def backward(n):
        ks = blocks[n]
        s_buf[...] = contract_cols(stacked(g_got, ks), values)
        for start in range(0, s_buf.shape[0], 16):
            now = slice(start, start + 16)
            prob = p_buf[n, now, :]
            d_prob = s_buf[now, :]
            delta = jnp.sum(prob * d_prob, axis=1, keepdims=True)
            b_buf[now, :] = (prob * (d_prob - delta) * scale).astype(bf)
        d_score = b_buf[...]
        d_query = dot_plain(d_score, keys).astype(bf)
        halves(dk_acc, dot_rows(d_score, stacked(q_buf, ks)), n)
        return deal(d_query, ks, dq_send, dq_own, dq_s, dq_r)

    def finish(acc, pair, copy, slots, own, s, r):
        copy.wait_recv()
        total = (acc[c] + pair[...]).astype(bf)
        for h in range(H):
            slots[h] = total[h * rows:(h + 1) * rows]
        own[:, cols] = slots[z]
        return total, [
            send(
                slots.at[lax.rem(z + k, H)], own.at[:, cols], s.at[k - 1], r.at[k - 1], head_dev(k)
            )
            for k in range(1, H)
        ]

    def split(ref, value, at=None):
        value = value.reshape(F, H, 2, -1, value.shape[1])
        for j in range(2):
            if at is None:
                ref[j] = value[:, :, j].astype(bf)
            else:
                ref[j, :, :, :, at * HD:(at + 1) * HD] = value[:, :, j].astype(bf)

    def over_clips(kept, got, out, slots, s, r):
        out[...] = (kept[c].astype(f32) + got[...].astype(f32)).astype(bf)
        return [
            send(out.at[lax.rem(f + k, F)], slots.at[k - 1], s.at[k - 1], r.at[k - 1], clip_dev(k))
            for k in range(1, F)
        ]

    def summed(copies, out, slots):
        total = out[f].astype(f32)
        for k in range(1, F):
            copies[k - 1].wait_recv()
            total = total + slots[k - 1].astype(f32)
        return total.astype(bf)

    dq_copies += backward(0)
    for copy in at_copies:
        copy.wait_recv()
    attention = att_own[...]
    split(go0, dot_rows(attention, dy_own[...]))
    pair_go = send(go0.at[other], go0_got, pair_s.at[1], pair_r.at[1], pair_dev)
    d_value, dv_copies = finish(dv_acc, dv_pair, pair_dv, dv_send, dv_own, dv_s, dv_r)
    dq_copies += backward(1)
    pair_dk = send(dk_acc.at[other], dk_pair, pair_s.at[2], pair_r.at[2], pair_dev)

    split(gv0, dot_plain(xt[...], d_value))
    pair_gv = send(gv0.at[other], gv0_got, pair_s.at[3], pair_r.at[3], pair_dev)
    pair_go.wait_recv()
    go_copies = over_clips(go0, go0_got, go1, go1_got, go1_s, go1_r)
    split(gw0, dot_plain(xt[...], dq_send[...].reshape(H * rows, HD)), 0)
    d_key, dk_copies = finish(dk_acc, dk_pair, pair_dk, dk_send, dk_own, dk_s, dk_r)
    split(gw0, dot_plain(xt[...], d_key), 1)
    pair_gw = send(gw0.at[other], gw0_got, pair_s.at[4], pair_r.at[4], pair_dev)
    late = w_forward(2)
    pair_gv.wait_recv()
    gv_copies = over_clips(gv0, gv0_got, gv1, gv1_got, gv1_s, gv1_r)
    late += w_forward(3)
    mixed_ref[...] = (xg[c, z].astype(f32) + dot_plain(attention, wo_all[...])).astype(bf)
    pair_gw.wait_recv()
    gw_copies = over_clips(gw0, gw0_got, gw1, gw1_got, gw1_s, gw1_r)

    late_key = w_forward(1)
    for copy in late + dv_copies + dq_copies:
        copy.wait_recv()
    token = dy_own[...].astype(f32) + contract_cols(dv_own[...], wv_all[...])
    token = token + contract_cols(dq_own[...], wq_all[...])
    for copy in late_key + dk_copies:
        copy.wait_recv()
    token_ref[...] = (token + contract_cols(dk_own[...], wk_all[...])).astype(bf)

    def to_owner(ref, got, s, r):
        got[z] = ref[z]
        return [
            send(ref.at[lax.rem(z + k, H)], got.at[z], s.at[k - 1], r.at[k - 1], head_dev(k))
            for k in range(1, H)
        ]

    go2[...] = summed(go_copies, go1, go1_got)
    last = to_owner(go2, go2_got, go2_s, go2_r)
    gv2[...] = summed(gv_copies, gv1, gv1_got)
    last += to_owner(gv2, gv2_got, gv2_s, gv2_r)
    gw2[...] = summed(gw_copies, gw1, gw1_got)
    last += to_owner(gw2, gw2_got, gw2_s, gw2_r)
    for copy in last:
        copy.wait_recv()
    total = go2_got[0].astype(f32)
    for h in range(1, H):
        total = total + go2_got[h].astype(f32)
    go_ref[...] = total
    for h in range(H):
        piece = gw2_got[h].astype(f32)
        gq_ref[:, h * HD:(h + 1) * HD] = piece[:, :HD]
        gk_ref[:, h * HD:(h + 1) * HD] = piece[:, HD:]
        gv_ref[:, h * HD:(h + 1) * HD] = gv2_got[h].astype(f32)
    for copy in started:
        copy.wait_send()
    for can_send, can_recv, out, _, pair, _ in flows.values():
        pl.when(can_send)(out.wait_send)
        pl.when(can_recv)(pair.wait_send)


def store_kernel(*refs):
    n = (len(refs) - 2) // 3
    srcs, outs, held = refs[:n], refs[n:2 * n], refs[2 * n:3 * n]
    sems_in, sems_out = refs[-2:]
    loads = [pltpu.make_async_copy(srcs[i], held[i], sems_in.at[i]) for i in range(n)]
    stores = [pltpu.make_async_copy(held[i], outs[i], sems_out.at[i]) for i in range(n)]
    for load in loads:
        load.start()
    for load, store in zip(loads, stores):
        load.wait()
        store.start()
    for store in stores:
        store.wait()


def fused_body(F, tokens, cotangent, w_query, w_key, w_value, w_out, block_mask, span_order):
    H = HEADS
    bf, f32 = jnp.bfloat16, jnp.float32
    x_rows, dy_rows = tokens[0], cotangent[0]
    rows, D = x_rows.shape
    HQ = w_query.shape[1]
    gq_rows = D // (F * H * 2)
    go_rows = HQ // (F * H * 2)
    V = pltpu.VMEM
    dma = pltpu.SemaphoreType.DMA
    hr = H * rows
    scratch = [
        V((2, H, rows, D), bf), V((rows, D), bf), V((D, HQ), bf), V((D, HQ), bf), V((D, HQ), bf), V((HQ, D), bf),
        V((D, 3 * HD), bf), V((hr // SPAN, 2 * hr), f32), V((H, rows, HD), bf), V((H, rows, HD), bf),
        V((2, H, rows, 2 * HD), bf), V((H, rows, HD), bf),
    ]
    for _ in range(4):
        scratch += [V((H, rows, HD), bf), V((rows, HQ), bf)]
    scratch += [
        V((2, hr // 2, 2 * hr), f32), V((hr // 2, 2 * hr), f32), V((hr // 2, 2 * hr), bf),
    ]
    for _ in range(2):
        scratch += [V((2, hr, HD), f32), V((hr, HD), f32)]
    scratch.append(V((D, hr), bf))
    for n, wide in ((go_rows, D), (gq_rows, HD), (gq_rows, 2 * HD)):
        scratch += [
            V((2, F, H, n, wide), bf), V((F, H, n, wide), bf), V((F, H, n, wide), bf),
            V((F - 1, H, n, wide), bf), V((H, n, wide), bf), V((H, n, wide), bf),
        ]
    scratch.append(dma((9,)))
    head, clip = (H - 1,), (F - 1,)
    for shape in (
        (2, H - 1), (2, H - 1), (4, F - 1), (4, F - 1), (3, F - 1), (3, F - 1), (1,),
        head, head, head, head, head, (5,), clip, head, clip, head, clip, head,
    ):
        scratch += [dma(shape), dma(shape)]
    vmem = pl.BlockSpec(memory_space=pltpu.VMEM)
    smem = pl.BlockSpec(memory_space=pltpu.SMEM)
    results = pl.pallas_call(
        functools.partial(fused_kernel, F),
        out_shape=(
            jax.ShapeDtypeStruct((rows, D), bf), jax.ShapeDtypeStruct((rows, D), bf),
            jax.ShapeDtypeStruct((gq_rows, HQ), f32), jax.ShapeDtypeStruct((gq_rows, HQ), f32),
            jax.ShapeDtypeStruct((gq_rows, HQ), f32), jax.ShapeDtypeStruct((go_rows, D), f32),
        ),
        in_specs=[pl.BlockSpec(memory_space=pltpu.HBM)] * 6 + [smem] * 2,
        out_specs=tuple([vmem] * 6),
        scratch_shapes=scratch,
        compiler_params=pltpu.CompilerParams(
            collective_id=0, has_side_effects=True, vmem_limit_bytes=60 * 1024 * 1024
        ),
        cost_estimate=pl.CostEstimate(
            flops=3 * 10**9, bytes_accessed=4 * 10**6, transcendentals=10**6
        ),
    )(x_rows, dy_rows, w_query, w_key, w_value, w_out, block_mask, span_order)
    mixed, token, gq, gk, gv, go = pl.pallas_call(
        store_kernel,
        out_shape=tuple(jax.ShapeDtypeStruct(r.shape, r.dtype) for r in results),
        in_specs=[pl.BlockSpec(memory_space=pltpu.HBM)] * 6,
        out_specs=tuple([pl.BlockSpec(memory_space=pltpu.HBM)] * 6),
        scratch_shapes=[V(r.shape, r.dtype) for r in results] + [dma((6,)), dma((6,))],
        compiler_params=pltpu.CompilerParams(vmem_limit_bytes=60 * 1024 * 1024),
    )(*results)
    return (mixed[None], token[None], gq, gk, gv, go)


def solution(mesh):
    shape = dict(mesh.shape)
    chosen = body
    if shape["ctx"] == 2 * HEADS and shape["fsdp"] == 4:
        chosen = functools.partial(fused_body, shape["fsdp"])
    return jax.shard_map(
        chosen,
        mesh=mesh,
        in_specs=(
            P("fsdp", "ctx", None),
            P("fsdp", "ctx", None),
            P("fsdp", None),
            P("fsdp", None),
            P("fsdp", None),
            P("fsdp", None),
            P(),
            P(),
        ),
        out_specs=(
            P("fsdp", "ctx", None),
            P("fsdp", "ctx", None),
            P(("fsdp", "ctx"), None),
            P(("fsdp", "ctx"), None),
            P(("fsdp", "ctx"), None),
            P(("fsdp", "ctx"), None),
        ),
        check_vma=False,
    )
```

```python
import functools
import math

import jax
import jax.numpy as jnp
from jax import lax
from jax.experimental import pallas as pl
from jax.experimental.pallas import tpu as pltpu
from jax.sharding import PartitionSpec as P

HEADS = 4
HD = 128
BLK = 128
SPAN = 64


NEG = -1e30
HIGH = lax.Precision.HIGHEST


def block_ids(span_order, start, count):
    rows = start + jnp.arange(count, dtype=jnp.int32)
    span = rows // SPAN
    lanes = jnp.arange(span_order.shape[0], dtype=jnp.int32)
    first = jnp.sum(jnp.where(span[:, None] == lanes[None, :], span_order[None, :], 0), axis=1)
    return (first * SPAN + rows % SPAN) // BLK


def allowed_between(mask_f, row_ids, col_ids):
    lanes = jnp.arange(mask_f.shape[0], dtype=jnp.int32)
    left = (row_ids[:, None] == lanes[None, :]).astype(jnp.float32)
    right = (col_ids[:, None] == lanes[None, :]).astype(jnp.float32)
    linked = jnp.dot(jnp.dot(left, mask_f), right.T)
    return linked > 0.5


def over_blocks(step, carry, pieces):
    count = pieces[0].shape[0]
    width = 512
    stacked = tuple((piece.reshape((count // width, width) + piece.shape[1:]) for piece in pieces))

    def scan_step(state, item):
        number, parts = item
        return (step(state, parts, number * width), None)

    numbers = jnp.arange(count // width, dtype=jnp.int32)
    carry, _ = lax.scan(scan_step, carry, (numbers, stacked))
    return carry


def contract_rows(left, right):
    return lax.dot_general(
        left, right, (((0,), (0,)), ((), ())), preferred_element_type=jnp.float32
    )


def contract_cols(left, right):
    return lax.dot_general(
        left, right, (((1,), (1,)), ((), ())), preferred_element_type=jnp.float32
    )


def body(tokens, cotangent, w_query, w_key, w_value, w_out, block_mask, span_order):
    x_rows = tokens[0]
    dy_rows = cotangent[0]
    rows = x_rows.shape[0]
    scale = 1.0 / math.sqrt(HD)
    full_q, full_k, full_v, full_o = (
        lax.all_gather(w_query, "fsdp", axis=0, tiled=True),
        lax.all_gather(w_key, "fsdp", axis=0, tiled=True),
        lax.all_gather(w_value, "fsdp", axis=0, tiled=True),
        lax.all_gather(w_out, "fsdp", axis=0, tiled=True),
    )
    query = jnp.dot(x_rows, full_q, preferred_element_type=jnp.float32).astype(jnp.bfloat16)
    keys = jnp.dot(x_rows, full_k, preferred_element_type=jnp.float32).astype(jnp.bfloat16)
    values = jnp.dot(x_rows, full_v, preferred_element_type=jnp.float32).astype(jnp.bfloat16)
    d_attn = contract_cols(dy_rows, full_o).astype(jnp.bfloat16)
    mask_f = block_mask.astype(jnp.float32)
    own_ids = block_ids(span_order, lax.axis_index("ctx") * rows, rows)
    q_own = query.reshape(rows, HEADS, HD)
    k_own = keys.reshape(rows, HEADS, HD)
    v_own = values.reshape(rows, HEADS, HD)
    g_own = d_attn.reshape(rows, HEADS, HD)

    def sweep_keys(carry, parts, start):
        top, total, out_acc, mix_acc, key_acc, dot_acc = carry
        count = parts[0].shape[0]
        k_part = parts[0].reshape(count, HEADS, HD)
        v_part = parts[1].reshape(count, HEADS, HD)
        keep = allowed_between(mask_f, own_ids, block_ids(span_order, start, count))[None]
        score = (
            jnp.einsum("qhd,khd->hqk", q_own, k_part, preferred_element_type=jnp.float32) * scale
        )
        score = jnp.where(keep, score, NEG)
        new_top = jnp.maximum(top, jnp.max(score, axis=-1))
        fade = jnp.exp(top - new_top)
        prob = jnp.where(keep, jnp.exp(score - new_top[:, :, None]), 0.0)
        k_wide = k_part.astype(jnp.float32)
        v_wide = v_part.astype(jnp.float32)
        total = fade * total + jnp.sum(prob, axis=-1)
        out_acc = fade[:, :, None] * out_acc + jnp.einsum(
            "hqk,khd->hqd", prob, v_wide, precision=HIGH
        )
        d_prob = jnp.einsum("qhd,khd->hqk", g_own, v_part, preferred_element_type=jnp.float32)
        weighted = prob * d_prob
        dot_acc = fade * dot_acc + jnp.sum(weighted, axis=-1)
        mix_acc = fade[:, :, None] * mix_acc + jnp.einsum(
            "hqk,khd->hqd", weighted, k_wide, precision=HIGH
        )
        key_acc = fade[:, :, None] * key_acc + jnp.einsum(
            "hqk,khd->hqd", prob, k_wide, precision=HIGH
        )
        return (new_top, total, out_acc, mix_acc, key_acc, dot_acc)

    flat = jnp.zeros((HEADS, rows), jnp.float32)
    cube = jnp.zeros((HEADS, rows, HD), jnp.float32)
    begin = (jnp.full((HEADS, rows), NEG, jnp.float32), flat, cube, cube, cube, flat)
    top, total, out_acc, mix_acc, key_acc, dot_acc = over_blocks(
        sweep_keys,
        begin,
        (
            lax.all_gather(keys, "ctx", axis=0, tiled=True),
            lax.all_gather(values, "ctx", axis=0, tiled=True),
        ),
    )
    share = 1.0 / total
    combined = out_acc * share[:, :, None]
    log_total = top + jnp.log(total)
    attention = jnp.transpose(combined, (1, 0, 2)).reshape(rows, HEADS * HD).astype(jnp.bfloat16)
    mixed = (
        x_rows.astype(jnp.float32) + jnp.dot(attention, full_o, preferred_element_type=jnp.float32)
    ).astype(jnp.bfloat16)
    delta = dot_acc * share
    log_rows = jnp.transpose(log_total)
    delta_rows = jnp.transpose(delta)

    def key_side(acc, parts, start):
        d_key, d_value = acc
        count = parts[0].shape[0]
        q_part = parts[0].reshape(count, HEADS, HD)
        g_part = parts[1].reshape(count, HEADS, HD)
        lse_part = jnp.transpose(parts[2])
        delta_part = jnp.transpose(parts[3])
        keep = allowed_between(mask_f, block_ids(span_order, start, count), own_ids)[None]
        score = (
            jnp.einsum("khd,qhd->hkq", q_part, k_own, preferred_element_type=jnp.float32) * scale
        )
        score = jnp.where(keep, score, NEG)
        prob = jnp.where(keep, jnp.exp(score - lse_part[:, :, None]), 0.0)
        d_prob = jnp.einsum("khd,qhd->hkq", g_part, v_own, preferred_element_type=jnp.float32)
        d_score = prob * (d_prob - delta_part[:, :, None])
        d_key = d_key + scale * jnp.einsum(
            "hkq,khd->hqd", d_score, q_part.astype(jnp.float32), precision=HIGH
        )
        d_value = d_value + jnp.einsum(
            "hkq,khd->hqd", prob, g_part.astype(jnp.float32), precision=HIGH
        )
        return (d_key, d_value)

    d_query = scale * (mix_acc - delta[:, :, None] * key_acc) * share[:, :, None]
    d_key, d_value = over_blocks(
        key_side,
        (cube, cube),
        (
            lax.all_gather(query.astype(jnp.float32), "ctx", axis=0, tiled=True).astype(
                jnp.bfloat16
            ),
            lax.all_gather(d_attn.astype(jnp.float32), "ctx", axis=0, tiled=True).astype(
                jnp.bfloat16
            ),
            lax.all_gather(log_rows, "ctx", axis=0, tiled=True),
            lax.all_gather(delta_rows, "ctx", axis=0, tiled=True),
        ),
    )

    def to_rows(grad_heads):
        return jnp.transpose(grad_heads, (1, 0, 2)).reshape(rows, HEADS * HD).astype(jnp.bfloat16)

    dq_rows = to_rows(d_query)
    dk_rows = to_rows(d_key)
    dv_rows = to_rows(d_value)
    token_grad = (
        dy_rows.astype(jnp.float32)
        + contract_cols(dq_rows, full_q)
        + contract_cols(dk_rows, full_k)
        + contract_cols(dv_rows, full_v)
    ).astype(jnp.bfloat16)
    grad_q = contract_rows(x_rows, dq_rows)
    grad_k = contract_rows(x_rows, dk_rows)
    grad_v = contract_rows(x_rows, dv_rows)
    grad_o = contract_rows(attention, dy_rows)
    grad_q, grad_k, grad_v, grad_o = (
        lax.psum_scatter(grad_q, ("fsdp", "ctx"), scatter_dimension=0, tiled=True),
        lax.psum_scatter(grad_k, ("fsdp", "ctx"), scatter_dimension=0, tiled=True),
        lax.psum_scatter(grad_v, ("fsdp", "ctx"), scatter_dimension=0, tiled=True),
        lax.psum_scatter(grad_o, ("fsdp", "ctx"), scatter_dimension=0, tiled=True),
    )
    return (mixed[None], token_grad[None], grad_q, grad_k, grad_v, grad_o)


def dot_rows(left, right):
    return lax.dot_general(
        left, right, (((0,), (0,)), ((), ())), preferred_element_type=jnp.float32
    )


def dot_plain(left, right):
    return jnp.dot(left, right, preferred_element_type=jnp.float32)


def fused_kernel(
    F,
    x_ref, dy_ref, wq_ref, wk_ref, wv_ref, wo_ref, mask_ref, order_ref,
    mixed_ref, token_ref, gq_ref, gk_ref, gv_ref, go_ref,
    xg, dy_own, wq_all, wk_all, wv_all, wo_all, wh, bias, g_send, g_got, kv_buf, q_buf,
    att_send, att_own, dq_send, dq_own, dk_send, dk_own, dv_send, dv_own,
    p_buf, s_buf, b_buf, dk_acc, dk_pair, dv_acc, dv_pair, xt,
    go0, go0_got, go1, go1_got, go2, go2_got,
    gv0, gv0_got, gv1, gv1_got, gv2, gv2_got,
    gw0, gw0_got, gw1, gw1_got, gw2, gw2_got,
    here, x_s, x_r, xf_s, xf_r, w_s, w_r, wf_s, wf_r, wh_s, wh_r, whf_s, whf_r,
    own_s, own_r, g_s, g_r, at_s, at_r, dq_s, dq_r,
    dk_s, dk_r, dv_s, dv_r, pair_s, pair_r, go1_s, go1_r, go2_s, go2_r,
    gv1_s, gv1_r, gv2_s, gv2_r, gw1_s, gw1_r, gw2_s, gw2_r,
):
    H = HEADS
    f = lax.axis_index("fsdp")
    ctx = lax.axis_index("ctx")
    z = ctx // 2
    c = ctx % 2
    other = 1 - c
    rows = x_ref.shape[0]
    bf = jnp.bfloat16
    f32 = jnp.float32
    scale = 1.0 / math.sqrt(HD)

    pair_dev = (f, z * 2 + other)

    def head_dev(k):
        return (f, lax.rem(z + k, H) * 2 + c)

    def clip_dev(k):
        return (lax.rem(f + k, F), ctx)

    started = []

    def remote(src, dst, s, r, dev):
        return pltpu.make_async_remote_copy(
            src_ref=src, dst_ref=dst, send_sem=s, recv_sem=r,
            device_id=dev, device_id_type=pl.DeviceIdType.MESH,
        )

    def send(src, dst, s, r, dev):
        copy = remote(src, dst, s, r, dev)
        copy.start()
        started.append(copy)
        return copy

    cols = pl.ds(pl.multiple_of(z * HD, HD), HD)
    weights = ((wo_ref, wo_all), (wk_ref, wk_all), (wv_ref, wv_all), (wq_ref, wq_all))
    heads = ((wk_ref, 0), (wv_ref, 1), (wq_ref, 2))

    def shard(i, owner):
        n = weights[i][0].shape[0]
        return weights[i][1].at[pl.ds(pl.multiple_of(owner * n, n), n)]

    shard_rows = wk_ref.shape[0]
    half_rows = shard_rows // 2

    def head_rows(i, owner, part):
        start = pl.multiple_of(owner * shard_rows + part * half_rows, half_rows)
        return wh.at[pl.ds(start, half_rows), pl.ds(i * HD, HD)]

    moves = [(x_ref, xg.at[c, z]), (dy_ref, dy_own)]
    moves += [(weights[i][0], shard(i, f)) for i in range(4)]
    moves += [
        (ref.at[:, cols], wh.at[pl.ds(pl.multiple_of(f * shard_rows, shard_rows), shard_rows), pl.ds(i * HD, HD)])
        for ref, i in heads
    ]
    local = [pltpu.make_async_copy(a, b, here.at[n]) for n, (a, b) in enumerate(moves)]
    for copy in local:
        copy.start()

    barrier = pltpu.get_barrier_semaphore()
    peers = [pair_dev] + [head_dev(k) for k in range(1, H)] + [clip_dev(k) for k in range(1, F)]
    for dev in peers:
        pl.semaphore_signal(barrier, inc=1, device_id=dev, device_id_type=pl.DeviceIdType.MESH)
    pl.semaphore_wait(barrier, len(peers))

    def flow(side, s):
        step = 1 if side == 0 else -1
        sent = z - step * s
        got = z - step * (s + 1)
        inside = (sent >= 0) & (sent <= H - 1)
        can_send = inside & (z < H - 1 if side == 0 else z > 0)
        can_recv = (got >= 0) & (got <= H - 1)
        src = x_ref if s == 0 else xg.at[c, sent]
        out = remote(src, xg.at[c, sent], x_s.at[side, s], x_r.at[side, s], (f, (z + step) * 2 + c))
        into = remote(src, xg.at[c, got], x_s.at[side, s], x_r.at[side, s], (f, (z + step) * 2 + c))
        part = xg.at[c, got]
        pair = remote(part, part, xf_s.at[side, s], xf_r.at[side, s], pair_dev)
        return can_send, can_recv, out, into, pair, got

    flows = {(side, s): flow(side, s) for s in range(H - 1) for side in range(2)}

    for side in range(2):
        can_send, _, out, _, _, _ = flows[side, 0]
        pl.when(can_send)(out.start)
    x_own = send(x_ref, xg.at[c, z], own_s.at[0], own_r.at[0], pair_dev)

    wh_copies = {}
    for ref, i in heads:
        src = ref.at[pl.ds(pl.multiple_of(c * half_rows, half_rows), half_rows), cols]
        for k in range(1, F):
            wh_copies[i, k] = send(
                src, head_rows(i, f, c), wh_s.at[i, k - 1], wh_r.at[i, k - 1], clip_dev(k)
            )

    def half_of(i, owner, part):
        n = weights[i][0].shape[0]
        start = pl.multiple_of(owner * n + part * (n // 2), n // 2)
        return weights[i][1].at[pl.ds(start, n // 2)]

    def w_send(i):
        ref = weights[i][0]
        n = ref.shape[0] // 2
        src = ref.at[pl.ds(pl.multiple_of(c * n, n), n)]
        return [
            send(src, half_of(i, f, c), w_s.at[i, k - 1], w_r.at[i, k - 1], clip_dev(k))
            for k in range(1, F)
        ]

    w_copies = {0: w_send(0)}
    for i in (2, 3, 1):
        w_copies[i] = w_send(i)

    def w_forward(i):
        out = []
        for k in range(1, F):
            w_copies[i][k - 1].wait_recv()
            part = half_of(i, lax.rem(f + F - k, F), c)
            out.append(send(part, part, wf_s.at[i, k - 1], wf_r.at[i, k - 1], pair_dev))
        return out

    spans = rows // SPAN
    per_block = BLK // SPAN
    width = bias.shape[1]
    place = lax.broadcasted_iota(jnp.int32, (1, width), 1) // SPAN
    key_block = [
        order_ref[(2 * h + j) * spans + s] // per_block
        for j in range(2) for h in range(H) for s in range(spans)
    ]
    for h in range(H):
        for s in range(spans):
            block = order_ref[(2 * h + c) * spans + s] // per_block
            line = jnp.full((1, width), NEG, f32)
            for n, key in enumerate(key_block):
                open_to = jnp.where(mask_ref[block, key] == 1, 0.0, NEG).astype(f32)
                line = jnp.where(place == n, open_to, line)
            bias[h * spans + s:h * spans + s + 1, :] = line

    for copy in local:
        copy.wait()

    forwards = []
    for k in range(1, F):
        for _, i in heads:
            wh_copies[i, k].wait_recv()
            part = head_rows(i, lax.rem(f + F - k, F), c)
            forwards.append(send(part, part, whf_s.at[i, k - 1], whf_r.at[i, k - 1], pair_dev))

    def pass_on(s):
        for side in range(2):
            _, can_recv, _, into, pair, _ = flows[side, s]

            @pl.when(can_recv)
            def _():
                into.wait_recv()
                pair.start()

            if s < H - 2:
                can_send, _, out, _, _, _ = flows[side, s + 1]
                pl.when(can_send)(out.start)

    def project_own(slot):
        out = dot_plain(xg[c, slot], wh[...]).astype(bf)
        kv_buf[c, slot] = out[:, :2 * HD]
        q_buf[slot] = out[:, 2 * HD:]
        xt[:, pl.ds(pl.multiple_of(slot * rows, rows), rows)] = xg[c, slot].T

    def project_pair(slot):
        kv_buf[other, slot] = dot_plain(xg[other, slot], wh[:, :2 * HD]).astype(bf)

    def project(s):
        for side in range(2):
            _, can_recv, _, _, pair, got = flows[side, s]

            @pl.when(can_recv)
            def _():
                project_own(got)
                pair.wait_recv()
                project_pair(got)

    pass_on(0)
    wo_forwards = w_forward(0)
    for copy in forwards:
        copy.wait_recv()
    project_own(z)
    x_own.wait_recv()
    project_pair(z)
    pass_on(1)
    for copy in wo_forwards:
        copy.wait_recv()
    g_all = contract_cols(dy_own[...], wo_all[...]).astype(bf)
    for h in range(H):
        g_send[h] = g_all[:, h * HD:(h + 1) * HD]
    g_copies = []
    for k in range(1, H):
        to = lax.rem(z + k, H)
        g_copies.append(send(g_send.at[to], g_got.at[z], g_s.at[k - 1], g_r.at[k - 1], head_dev(k)))
    g_got[z] = g_send[z]
    project(0)
    project(1)
    pass_on(2)
    project(2)
    for copy in g_copies:
        copy.wait_recv()

    kv = kv_buf[...].reshape(2 * H * rows, 2 * HD)
    keys = kv[:, :HD]
    values = kv[:, HD:]
    blocks = ((1, 2), (3, 0))

    def slots_of(ks):
        return [lax.rem(z + k, H) for k in ks]

    def stacked(buf, ks):
        return jnp.concatenate([buf[h] for h in slots_of(ks)], axis=0)

    def deal(value, ks, slots, own, s, r):
        out = []
        for n, (k, h) in enumerate(zip(ks, slots_of(ks))):
            piece = value[n * rows:(n + 1) * rows]
            slots[h] = piece
            if k == 0:
                own[:, cols] = piece
            else:
                out.append(send(slots.at[h], own.at[:, cols], s.at[k - 1], r.at[k - 1], head_dev(k)))
        return out

    def halves(ref, value, n):
        value = value.reshape(2, H * rows, HD)
        ref[...] = value if n == 0 else ref[...] + value

    at_copies = []
    for n, ks in enumerate(blocks):
        s_buf[...] = contract_cols(stacked(q_buf, ks), keys)
        lines = [bias[pl.ds(h * spans + s, 1), :] for h in slots_of(ks) for s in range(spans)]
        for start in range(0, s_buf.shape[0], 16):
            now = slice(start, start + 16)
            score = s_buf[now, :] * scale + lines[start // SPAN]
            prob = jnp.exp(score - jnp.max(score, axis=1, keepdims=True))
            prob = prob * (1.0 / jnp.sum(prob, axis=1, keepdims=True))
            p_buf[n, now, :] = prob
            b_buf[now, :] = prob.astype(bf)
        prob_b = b_buf[...]
        at_copies += deal(dot_plain(prob_b, values).astype(bf), ks, att_send, att_own, at_s, at_r)
        halves(dv_acc, dot_rows(prob_b, stacked(g_got, ks)), n)
    pair_dv = send(dv_acc.at[other], dv_pair, pair_s.at[0], pair_r.at[0], pair_dev)

    dq_copies = []

    def backward(n):
        ks = blocks[n]
        s_buf[...] = contract_cols(stacked(g_got, ks), values)
        for start in range(0, s_buf.shape[0], 16):
            now = slice(start, start + 16)
            prob = p_buf[n, now, :]
            d_prob = s_buf[now, :]
            delta = jnp.sum(prob * d_prob, axis=1, keepdims=True)
            b_buf[now, :] = (prob * (d_prob - delta) * scale).astype(bf)
        d_score = b_buf[...]
        d_query = dot_plain(d_score, keys).astype(bf)
        halves(dk_acc, dot_rows(d_score, stacked(q_buf, ks)), n)
        return deal(d_query, ks, dq_send, dq_own, dq_s, dq_r)

    def finish(acc, pair, copy, slots, own, s, r):
        copy.wait_recv()
        total = (acc[c] + pair[...]).astype(bf)
        for h in range(H):
            slots[h] = total[h * rows:(h + 1) * rows]
        own[:, cols] = slots[z]
        return total, [
            send(
                slots.at[lax.rem(z + k, H)], own.at[:, cols], s.at[k - 1], r.at[k - 1], head_dev(k)
            )
            for k in range(1, H)
        ]

    def split(ref, value, at=None):
        value = value.reshape(F, H, 2, -1, value.shape[1])
        for j in range(2):
            if at is None:
                ref[j] = value[:, :, j].astype(bf)
            else:
                ref[j, :, :, :, at * HD:(at + 1) * HD] = value[:, :, j].astype(bf)

    def over_clips(kept, got, out, slots, s, r):
        out[...] = (kept[c].astype(f32) + got[...].astype(f32)).astype(bf)
        return [
            send(out.at[lax.rem(f + k, F)], slots.at[k - 1], s.at[k - 1], r.at[k - 1], clip_dev(k))
            for k in range(1, F)
        ]

    def summed(copies, out, slots):
        total = out[f].astype(f32)
        for k in range(1, F):
            copies[k - 1].wait_recv()
            total = total + slots[k - 1].astype(f32)
        return total.astype(bf)

    dq_copies += backward(0)
    for copy in at_copies:
        copy.wait_recv()
    attention = att_own[...]
    split(go0, dot_rows(attention, dy_own[...]))
    pair_go = send(go0.at[other], go0_got, pair_s.at[1], pair_r.at[1], pair_dev)
    d_value, dv_copies = finish(dv_acc, dv_pair, pair_dv, dv_send, dv_own, dv_s, dv_r)
    dq_copies += backward(1)
    pair_dk = send(dk_acc.at[other], dk_pair, pair_s.at[2], pair_r.at[2], pair_dev)

    split(gv0, dot_plain(xt[...], d_value))
    pair_gv = send(gv0.at[other], gv0_got, pair_s.at[3], pair_r.at[3], pair_dev)
    pair_go.wait_recv()
    go_copies = over_clips(go0, go0_got, go1, go1_got, go1_s, go1_r)
    split(gw0, dot_plain(xt[...], dq_send[...].reshape(H * rows, HD)), 0)
    d_key, dk_copies = finish(dk_acc, dk_pair, pair_dk, dk_send, dk_own, dk_s, dk_r)
    split(gw0, dot_plain(xt[...], d_key), 1)
    pair_gw = send(gw0.at[other], gw0_got, pair_s.at[4], pair_r.at[4], pair_dev)
    late = w_forward(2)
    pair_gv.wait_recv()
    gv_copies = over_clips(gv0, gv0_got, gv1, gv1_got, gv1_s, gv1_r)
    late += w_forward(3)
    mixed_ref[...] = (xg[c, z].astype(f32) + dot_plain(attention, wo_all[...])).astype(bf)
    pair_gw.wait_recv()
    gw_copies = over_clips(gw0, gw0_got, gw1, gw1_got, gw1_s, gw1_r)

    late_key = w_forward(1)
    for copy in late + dv_copies + dq_copies:
        copy.wait_recv()
    token = dy_own[...].astype(f32) + contract_cols(dv_own[...], wv_all[...])
    token = token + contract_cols(dq_own[...], wq_all[...])
    for copy in late_key + dk_copies:
        copy.wait_recv()
    token_ref[...] = (token + contract_cols(dk_own[...], wk_all[...])).astype(bf)

    def to_owner(ref, got, s, r):
        got[z] = ref[z]
        return [
            send(ref.at[lax.rem(z + k, H)], got.at[z], s.at[k - 1], r.at[k - 1], head_dev(k))
            for k in range(1, H)
        ]

    go2[...] = summed(go_copies, go1, go1_got)
    last = to_owner(go2, go2_got, go2_s, go2_r)
    gv2[...] = summed(gv_copies, gv1, gv1_got)
    last += to_owner(gv2, gv2_got, gv2_s, gv2_r)
    gw2[...] = summed(gw_copies, gw1, gw1_got)
    last += to_owner(gw2, gw2_got, gw2_s, gw2_r)
    for copy in last:
        copy.wait_recv()
    total = go2_got[0].astype(f32)
    for h in range(1, H):
        total = total + go2_got[h].astype(f32)
    go_ref[...] = total
    for h in range(H):
        piece = gw2_got[h].astype(f32)
        gq_ref[:, h * HD:(h + 1) * HD] = piece[:, :HD]
        gk_ref[:, h * HD:(h + 1) * HD] = piece[:, HD:]
        gv_ref[:, h * HD:(h + 1) * HD] = gv2_got[h].astype(f32)
    for copy in started:
        copy.wait_send()
    for can_send, can_recv, out, _, pair, _ in flows.values():
        pl.when(can_send)(out.wait_send)
        pl.when(can_recv)(pair.wait_send)


def store_kernel(*refs):
    n = (len(refs) - 2) // 3
    srcs, outs, held = refs[:n], refs[n:2 * n], refs[2 * n:3 * n]
    sems_in, sems_out = refs[-2:]
    loads = [pltpu.make_async_copy(srcs[i], held[i], sems_in.at[i]) for i in range(n)]
    stores = [pltpu.make_async_copy(held[i], outs[i], sems_out.at[i]) for i in range(n)]
    for load in loads:
        load.start()
    for load, store in zip(loads, stores):
        load.wait()
        store.start()
    for store in stores:
        store.wait()


def fused_body(F, tokens, cotangent, w_query, w_key, w_value, w_out, block_mask, span_order):
    H = HEADS
    bf, f32 = jnp.bfloat16, jnp.float32
    x_rows, dy_rows = tokens[0], cotangent[0]
    rows, D = x_rows.shape
    HQ = w_query.shape[1]
    gq_rows = D // (F * H * 2)
    go_rows = HQ // (F * H * 2)
    V = pltpu.VMEM
    dma = pltpu.SemaphoreType.DMA
    hr = H * rows
    scratch = [
        V((2, H, rows, D), bf), V((rows, D), bf), V((D, HQ), bf), V((D, HQ), bf), V((D, HQ), bf), V((HQ, D), bf),
        V((D, 3 * HD), bf), V((hr // SPAN, 2 * hr), f32), V((H, rows, HD), bf), V((H, rows, HD), bf),
        V((2, H, rows, 2 * HD), bf), V((H, rows, HD), bf),
    ]
    for _ in range(4):
        scratch += [V((H, rows, HD), bf), V((rows, HQ), bf)]
    scratch += [
        V((2, hr // 2, 2 * hr), f32), V((hr // 2, 2 * hr), f32), V((hr // 2, 2 * hr), bf),
    ]
    for _ in range(2):
        scratch += [V((2, hr, HD), f32), V((hr, HD), f32)]
    scratch.append(V((D, hr), bf))
    for n, wide in ((go_rows, D), (gq_rows, HD), (gq_rows, 2 * HD)):
        scratch += [
            V((2, F, H, n, wide), bf), V((F, H, n, wide), bf), V((F, H, n, wide), bf),
            V((F - 1, H, n, wide), bf), V((H, n, wide), bf), V((H, n, wide), bf),
        ]
    scratch.append(dma((9,)))
    head, clip = (H - 1,), (F - 1,)
    for shape in (
        (2, H - 1), (2, H - 1), (4, F - 1), (4, F - 1), (3, F - 1), (3, F - 1), (1,),
        head, head, head, head, head, (5,), clip, head, clip, head, clip, head,
    ):
        scratch += [dma(shape), dma(shape)]
    vmem = pl.BlockSpec(memory_space=pltpu.VMEM)
    smem = pl.BlockSpec(memory_space=pltpu.SMEM)
    results = pl.pallas_call(
        functools.partial(fused_kernel, F),
        out_shape=(
            jax.ShapeDtypeStruct((rows, D), bf), jax.ShapeDtypeStruct((rows, D), bf),
            jax.ShapeDtypeStruct((gq_rows, HQ), f32), jax.ShapeDtypeStruct((gq_rows, HQ), f32),
            jax.ShapeDtypeStruct((gq_rows, HQ), f32), jax.ShapeDtypeStruct((go_rows, D), f32),
        ),
        in_specs=[pl.BlockSpec(memory_space=pltpu.HBM)] * 6 + [smem] * 2,
        out_specs=tuple([vmem] * 6),
        scratch_shapes=scratch,
        compiler_params=pltpu.CompilerParams(
            collective_id=0, has_side_effects=True, vmem_limit_bytes=60 * 1024 * 1024
        ),
        cost_estimate=pl.CostEstimate(
            flops=3 * 10**9, bytes_accessed=4 * 10**6, transcendentals=10**6
        ),
    )(x_rows, dy_rows, w_query, w_key, w_value, w_out, block_mask, span_order)
    mixed, token, gq, gk, gv, go = pl.pallas_call(
        store_kernel,
        out_shape=tuple(jax.ShapeDtypeStruct(r.shape, r.dtype) for r in results),
        in_specs=[pl.BlockSpec(memory_space=pltpu.HBM)] * 6,
        out_specs=tuple([pl.BlockSpec(memory_space=pltpu.HBM)] * 6),
        scratch_shapes=[V(r.shape, r.dtype) for r in results] + [dma((6,)), dma((6,))],
        compiler_params=pltpu.CompilerParams(vmem_limit_bytes=60 * 1024 * 1024),
    )(*results)
    return (mixed[None], token[None], gq, gk, gv, go)


def solution(mesh):
    shape = dict(mesh.shape)
    chosen = body
    if shape["ctx"] == 2 * HEADS and shape["fsdp"] == 4:
        chosen = functools.partial(fused_body, shape["fsdp"])
    return jax.shard_map(
        chosen,
        mesh=mesh,
        in_specs=(
            P("fsdp", "ctx", None),
            P("fsdp", "ctx", None),
            P("fsdp", None),
            P("fsdp", None),
            P("fsdp", None),
            P("fsdp", None),
            P(),
            P(),
        ),
        out_specs=(
            P("fsdp", "ctx", None),
            P("fsdp", "ctx", None),
            P(("fsdp", "ctx"), None),
            P(("fsdp", "ctx"), None),
            P(("fsdp", "ctx"), None),
            P(("fsdp", "ctx"), None),
        ),
        check_vma=False,
    )
```
